32 devices in a mesh: row: 4 (over y, x), col: 8 (over z, core).
Axes of the slice: x: 2, y: 2, z: 4, core: 2. Of those that a mesh axis runs over, the one named last changes fastest.
Arguments:
- tokens: bfloat16 [4096, 2880], P(('col', 'row')), may hold values from -6 to 6
- seg_ids: int32 [4096], P(('col', 'row')), may hold values from 0 to 3, never falling along the last dimension, each value on 1 to 2048 neighbouring positions
- norm_gain: float32 [2880], replicated, may hold values from 0.1 to 1.9
- query_weight: bfloat16 [2880, 4096], P('col', 'row'), may hold values from -4.5839394 to 4.5839394
- kv_weight: bfloat16 [2880, 1024], P('col', 'row'), may hold values from -0.1118034 to 0.1118034
- out_weight: bfloat16 [4096, 2880], P('row', 'col'), may hold values from -0.09375 to 0.09375
- sinks: float32 [64], P('row'), may hold values from 1 to 6
- moe_gain: float32 [2880], replicated, may hold values from 0.1 to 1.9
- routes: int32 [4096, 4], P(('col', 'row')), may hold values from 0 to 63, all different within a row; in each aligned block of 128 rows (0 to 127, 128 to 255, ...) at most 9 rows name the same one
- route_weights: float32 [4096, 4], P(('col', 'row')), may hold values from 0.05 to 0.5
- expert_in: bfloat16 [128, 2880, 1536], P(('row', 'col')), may hold values from -0.109375 to 0.109375
- expert_out: bfloat16 [128, 768, 2880], P(('row', 'col')), may hold values from -0.21875 to 0.21875
Outputs:
- mixed: bfloat16 [4096, 2880], P(('col', 'row'))
- kv_cache: bfloat16 [4096, 1024], P('col', 'row')
The draws below stay inside these ranges and needn't reach their ends.
Inputs may be any that keep to these rules, and one draw needn't show every extreme that they name: `seg_ids`: never falling; each prompt has 1 to 2048 tokens, one exactly 2048. `routes`: each row names 4 different experts; among the 128 rows of one device no expert is named more than 9 times, and on some device one is named exactly 9 times.
All inputs are finite; a program needn't handle non-finite values.
Results may differ from the reference program's by a relative error of at most 0.012.
Values may be sent and summed in bfloat16 or wider, within the bound.
No kernel may reach another device: no remote copies, remote signals or barrier semaphores. Data moves between devices by JAX's collectives and lax.ppermute only.
A program may use at most 128 MiB of HBM per device.

```python
import math
import jax
import jax.numpy as jnp
import numpy as np
from jax import lax

D = 2880
HQ = 64
KVH = 8
HD = 64
WIN = 128
EXPERTS = 64
HALF = 768
TOP = 4
TOK_DEV = 128
CAP = 9
TOKENS = 4096
MAXLEN = 2048
SEGS = 4
N_ROW = 4
N_COL = 8


strength_list = (12.0, 24.0, 40.0)


def key_value_block(key):
    entries = jax.random.normal(jax.random.fold_in(key, 101), (D, KVH, 2, HD), jnp.float32)
    entries = jnp.clip(entries, -6.0, 6.0) * D ** (-0.5)
    return entries


def draw_kv_weight(key, part):
    return key_value_block(key).reshape(D, KVH * 2 * HD).astype(jnp.bfloat16)


def draw_query_weight(key, part):
    key_columns = key_value_block(key)[:, :, 0, :]
    per_head = jnp.repeat(key_columns, HQ // KVH, axis=1)
    spread_part = jnp.clip(jax.random.normal(jax.random.fold_in(key, 102), (D, HQ, HD), jnp.float32), -6.0, 6.0) * D ** (-0.5)
    head_order = jax.random.permutation(jax.random.fold_in(key, 103), HQ)
    strengths = jnp.zeros((HQ,), jnp.float32).at[head_order[:3]].set(jnp.array(strength_list, jnp.float32))
    turning = (jnp.arange(HD, dtype=jnp.int32) % (HD // 2) != 0).astype(jnp.float32)
    lifted = strengths[:, None] * turning[None, :]
    return (spread_part + lifted[None] * per_head).reshape(D, HQ * HD).astype(jnp.bfloat16)


def draw_tokens(key, part):
    base_rows = jnp.clip(jax.random.normal(jax.random.fold_in(key, 201), (TOKENS, D), jnp.float32), -6.0, 6.0)
    leading = base_rows[0::2]
    trailing = base_rows[1::2]
    kept_width = D - D // 4
    mirrored = jnp.concatenate([leading[:, :kept_width], jnp.flip(leading[:, kept_width:], axis=1)], axis=1)
    picked = jax.random.randint(jax.random.fold_in(key, 202), (TOKENS // 2, 1), 0, 8) == 0
    trailing = jnp.where(picked, mirrored, trailing)
    return jnp.stack([leading, trailing], axis=1).reshape(TOKENS, D).astype(jnp.bfloat16)


def shard_levels(rng, extent, cuts, least, largest):
    gain = 1.0
    for axis_at, shards_of in cuts:
        steps = jax.random.uniform(jax.random.fold_in(jax.random.fold_in(rng, 6), axis_at), (shards_of,), jnp.float32, least / len(cuts), largest / len(cuts))
        gain = gain * jnp.repeat(jnp.exp(steps), extent[axis_at] // shards_of).reshape((-1,) + (1,) * (len(extent) - 1 - axis_at))
    return gain


def profile(count, total, limit, lean):
    weights = [(1 << 20) // math.isqrt(rank ** lean) + 1 for rank in range(2, count + 1)]
    spare, given = total - limit - (count - 1), [1] * (count - 1)
    while spare > 0:
        candidates = [i for i in range(count - 1) if given[i] < limit]
        mass, budget = sum([weights[i] for i in candidates]), spare
        for i in candidates:
            extra = min(limit - given[i], max(1, budget * weights[i] // mass), spare)
            given[i] = given[i] + extra
            spare = spare - extra
    return np.array([limit] + given)


def uneven_parts(own_key, number_of, total, most, slope):
    if number_of == 2:
        one = jax.random.randint(own_key, (), max(1, total - most), min(most, total - 1) + 1)
        return jnp.stack([one, total - one])
    lengths = jnp.asarray(profile(number_of, total, most, slope), jnp.int32)
    couples = (number_of - 1) // 2
    source_of, taker = lengths[1:1 + 2 * couples:2], lengths[2:2 + 2 * couples:2]
    room = jnp.minimum(source_of - 1, most - taker)
    passed = jax.random.randint(jax.random.fold_in(own_key, 1), (couples,), 0, 1 << 20) % (room + 1)
    lengths = lengths.at[1:1 + 2 * couples:2].set(source_of - passed).at[2:2 + 2 * couples:2].set(taker + passed)
    return lengths[jax.random.permutation(jax.random.fold_in(own_key, 2), number_of)]


def deal_out(key, own, number, rows, amount, top, reach, lean):
    order = jax.random.permutation(key, amount)
    crowded, common = shares(amount, rows * top, reach, lean, True), shares(amount, rows * top, reach, lean, False)
    places = jnp.arange(amount)

    def named(sizes, turn):
        used = int((sizes > 0).sum())
        fixed = max(1, used // 4)
        shifted = fixed + (places - fixed + turn * (used - fixed)) % max(1, amount - fixed)
        return jnp.zeros((amount,), jnp.int32).at[order[jnp.where(places < fixed, places, shifted)]].set(jnp.asarray(sizes, jnp.int32))

    sizes = jnp.where(number % 4 == 0, named(crowded, number // 4), named(common, number - number // 4 - 1))
    mixed = jax.random.permutation(jax.random.fold_in(own, 3), amount)
    giver, receiver = mixed[0:amount // 2 * 2:2], mixed[1:amount // 2 * 2:2]
    slack = jnp.minimum(sizes[giver] - 1, reach - sizes[receiver]) // 2
    slack = jnp.where((giver == order[0]) | (receiver == order[0]) | (sizes[receiver] == 0), 0, jnp.maximum(slack, 0))
    shifted = jax.random.randint(jax.random.fold_in(own, 4), (amount // 2,), 0, 1 << 20) % (slack + 1)
    sizes = sizes.at[giver].add(-shifted).at[receiver].add(shifted)
    items = jnp.searchsorted(jnp.cumsum(sizes), jnp.arange(rows * top), side="right").astype(jnp.int32)
    grid = items.reshape(top, rows).T
    grid = grid[jax.random.permutation(jax.random.fold_in(own, 1), rows)]
    turn = jax.random.randint(jax.random.fold_in(own, 2), (rows, 1), 0, top)
    return jnp.take_along_axis(grid, (jnp.arange(top)[None, :] + turn) % top, axis=1)


def shares(amount, total, reach, lean, full):
    loads = [(1 << 20) // math.isqrt(grade ** lean) + 1 for grade in range(1, amount + 1)]
    largest = reach if full else min(reach, max(-(-total // amount), total * loads[0] // sum(loads)))
    least = 1 if total - largest >= amount - 1 else 0
    given, rest = [largest] + [least] * (amount - 1), total - largest - least * (amount - 1)
    while rest > 0:
        free = [i for i in range(1, amount) if given[i] < largest] or [i for i in range(1, amount) if given[i] < reach]
        mass, left = sum([loads[i] for i in free]), rest
        for i in free:
            more = min(reach - given[i], max(1, left * loads[i] // mass), rest)
            given[i] = given[i] + more
            rest = rest - more
    return np.array(given)


def scatter_about(key, dims, spread, bound, cuts=(), kind=jnp.bfloat16):
    values = spread * jax.random.normal(key, dims, jnp.float32)
    if cuts:
        values = values * shard_levels(key, dims, cuts, -0.22, 0.18)
    return jnp.clip(values, -bound, bound).astype(kind)


def setup_inputs(seed: int = 0) -> dict:
    key_list = jax.random.split(jax.random.key(seed), 13)
    tokens = draw_tokens(jax.random.fold_in(key_list[12], 71), 0)
    seg_ids = jnp.searchsorted(jnp.cumsum(uneven_parts(key_list[1], SEGS, TOKENS, MAXLEN, 2)), jnp.arange(TOKENS), side="right").astype(jnp.int32)
    norm_gain = jnp.clip(1.0 + 0.18 * jax.random.normal(key_list[2], (D,), jnp.float32), 0.1, 1.9)
    query_weight = draw_query_weight(jax.random.fold_in(key_list[12], 71), 0)
    kv_weight = draw_kv_weight(jax.random.fold_in(key_list[12], 71), 0)
    out_weight = scatter_about(key_list[5], (HQ * HD, D), (HQ * HD) ** -0.5, 0.09375, ((0, 4), (1, 8)))
    sinks = jnp.clip(1.0 + 5.0 * jax.random.uniform(key_list[6], (HQ,), jnp.float32) ** shard_levels(key_list[6], (HQ,), ((0, 4),), -0.2, 0.2), 1.0, 6.0)
    moe_gain = jnp.clip(1.0 + 0.18 * jax.random.normal(key_list[7], (D,), jnp.float32), 0.1, 1.9)
    routes_keys = jax.random.split(jax.random.fold_in(key_list[8], 1), TOKENS // TOK_DEV)
    routes_turns = jax.random.permutation(jax.random.fold_in(key_list[8], 3), TOKENS // TOK_DEV)
    routes = jax.vmap(lambda own, number: deal_out(jax.random.fold_in(key_list[8], 2), own, number, TOK_DEV, EXPERTS, TOP, CAP, 1))(routes_keys, routes_turns).reshape((TOKENS, TOP))
    route_weights = jnp.clip(0.05 + 0.45 * jax.random.uniform(key_list[9], (TOKENS, TOP), jnp.float32) ** shard_levels(key_list[9], (TOKENS, TOP), ((0, 32),), -0.2, 0.2), 0.05, 0.5)
    expert_in = scatter_about(key_list[10], (2 * EXPERTS, D, 2 * HALF), D ** -0.5, 0.109375, ((0, 32),))
    expert_out = scatter_about(key_list[11], (2 * EXPERTS, HALF, D), HALF ** -0.5, 0.21875, ((0, 32),))
    return {"tokens": tokens, "seg_ids": seg_ids, "norm_gain": norm_gain, "query_weight": query_weight, "kv_weight": kv_weight, "out_weight": out_weight, "sinks": sinks, "moe_gain": moe_gain, "routes": routes, "route_weights": route_weights, "expert_in": expert_in, "expert_out": expert_out}


eps_norm = 1e-05
theta_base = 150000.0
glu_alpha = 1.702
masked_score = -1e+30

def rms_scale(values_in, gain_vec):
    widened = values_in.astype(jnp.float32)
    return widened * lax.rsqrt(lax.optimization_barrier(jnp.mean(widened * widened, axis=-1, keepdims=True)) + eps_norm) * gain_vec

def rotate(values_in, positions):
    half_dim = values_in.shape[-1] // 2
    frequency = jnp.exp(jnp.arange(half_dim, dtype=jnp.float32) * (-2.0 * math.log(theta_base) / values_in.shape[-1]))
    angles = positions.astype(jnp.float32)[:, None] * frequency[None, :]
    cosine = jnp.cos(angles)[:, None, :]
    sine = jnp.sin(angles)[:, None, :]
    first_half = values_in[..., :half_dim]
    second_half = values_in[..., half_dim:]
    return jnp.concatenate([first_half * cosine - second_half * sine, second_half * cosine + first_half * sine], axis=-1)

def run_positions(segments):
    count_all = segments.shape[0]
    index_all = jnp.arange(count_all, dtype=jnp.int32)
    before = jnp.concatenate([jnp.full((1,), -1, jnp.int32), segments[:-1]])
    marks = jnp.where(segments != before, index_all, jnp.int32(0))
    return index_all - lax.cummax(marks)

def attend_tile(query_tile, key_tile, value_tile, query_seg, key_seg, query_pos, key_pos, sink_grid):
    scores = jnp.einsum('qkgd,lkd->kgql', query_tile, key_tile) * query_tile.shape[-1] ** (-0.5)
    distance = query_pos[:, None] - key_pos[None, :]
    allowed = (query_seg[:, None] == key_seg[None, :]) & (distance >= 0) & (distance < WIN) & (key_pos[None, :] >= 0)
    scores = jnp.where(allowed[None, None], scores, masked_score)
    sink_col = sink_grid[:, :, None]
    ceiling = jnp.maximum(lax.optimization_barrier(jnp.max(scores, axis=-1)), sink_col)
    expo = jnp.exp(scores - ceiling[..., None])
    denom = lax.optimization_barrier(jnp.sum(expo, axis=-1)) + jnp.exp(sink_col - ceiling)
    probs = (expo / denom[..., None]).astype(jnp.bfloat16)
    return jnp.einsum('kgql,lkd->qkgd', probs.astype(jnp.float32), value_tile).astype(jnp.bfloat16)

def attention_all(queries, keys, values, segments, sinks):
    group_size = HQ // KVH
    query_grid = queries.reshape(TOKENS // WIN, WIN, KVH, group_size, HD)
    key_padded = jnp.concatenate([jnp.zeros((WIN, KVH, HD), jnp.bfloat16), keys])
    value_padded = jnp.concatenate([jnp.zeros((WIN, KVH, HD), jnp.bfloat16), values])
    seg_padded = jnp.concatenate([jnp.full((WIN,), -1, jnp.int32), segments])
    sink_grid = sinks.reshape(KVH, group_size)

    def one_block(block_id):
        first_row = block_id * WIN
        query_tile = lax.dynamic_index_in_dim(query_grid, block_id, 0, keepdims=False).astype(jnp.float32)
        key_tile = lax.dynamic_slice_in_dim(key_padded, first_row, 2 * WIN, 0).astype(jnp.float32)
        value_tile = lax.dynamic_slice_in_dim(value_padded, first_row, 2 * WIN, 0).astype(jnp.float32)
        key_seg = lax.dynamic_slice_in_dim(seg_padded, first_row, 2 * WIN, 0)
        query_seg = lax.dynamic_slice_in_dim(segments, first_row, WIN, 0)
        query_pos = first_row + jnp.arange(WIN, dtype=jnp.int32)
        key_pos = first_row - WIN + jnp.arange(2 * WIN, dtype=jnp.int32)
        return attend_tile(query_tile, key_tile, value_tile, query_seg, key_seg, query_pos, key_pos, sink_grid)
    tiles = lax.map(one_block, jnp.arange(TOKENS // WIN, dtype=jnp.int32))
    return tiles.reshape(TOKENS, HQ * HD)

def experts_all(moe_in, routes, route_weights, expert_in, expert_out):
    route_flat = routes.reshape(-1)
    weight_flat = route_weights.reshape(-1)
    total_routes = route_flat.shape[0]
    ordering = jnp.argsort(route_flat, stable=True).astype(jnp.int32)
    expert_ids = jnp.arange(EXPERTS, dtype=jnp.int32)
    counts = lax.optimization_barrier(jnp.sum((route_flat[:, None] == expert_ids[None, :]).astype(jnp.int32), axis=0))
    offsets = jnp.cumsum(counts) - counts
    most_rows = N_ROW * N_COL * CAP

    def one_expert(running, expert):
        places = offsets[expert] + jnp.arange(most_rows, dtype=jnp.int32)
        valid = jnp.arange(most_rows, dtype=jnp.int32) < counts[expert]
        chosen = ordering[jnp.minimum(places, total_routes - 1)]
        token_ids = chosen // TOP
        rows_in = moe_in[token_ids]
        summed = jnp.zeros((most_rows, D), jnp.float32)
        for half_id in range(2):
            slice_id = 2 * expert + half_id
            mixed_in = jnp.dot(rows_in, expert_in[slice_id], preferred_element_type=jnp.float32)
            gate_part = mixed_in[:, :HALF]
            up_part = mixed_in[:, HALF:]
            hidden_act = (gate_part * jax.nn.sigmoid(glu_alpha * gate_part) * (up_part + 1.0)).astype(jnp.bfloat16)
            part_out = jnp.dot(hidden_act, expert_out[slice_id], preferred_element_type=jnp.float32).astype(jnp.bfloat16)
            part_out = lax.optimization_barrier(part_out)
            summed = summed + part_out.astype(jnp.float32)
        scaled = jnp.where(valid, weight_flat[chosen], jnp.float32(0.0))
        running = running.at[token_ids].add(scaled[:, None] * summed)
        return (running, None)
    result, _ = lax.scan(one_expert, jnp.zeros((TOKENS, D), jnp.float32), expert_ids)
    return result

def reference(tokens, seg_ids, norm_gain, query_weight, kv_weight, out_weight, sinks, moe_gain, routes, route_weights, expert_in, expert_out):
    normed = rms_scale(tokens, norm_gain).astype(jnp.bfloat16)
    positions = run_positions(seg_ids)
    query_raw = jnp.dot(normed, query_weight, preferred_element_type=jnp.float32).reshape(TOKENS, HQ, HD)
    queries = rotate(query_raw, positions).astype(jnp.bfloat16)
    kv_raw = jnp.dot(normed, kv_weight, preferred_element_type=jnp.float32).reshape(TOKENS, KVH, 2, HD)
    keys = rotate(kv_raw[:, :, 0], positions).astype(jnp.bfloat16)
    values = kv_raw[:, :, 1].astype(jnp.bfloat16)
    kv_cache = jnp.stack([keys, values], axis=2).reshape(TOKENS, KVH * 2 * HD)
    attended = attention_all(queries, keys, values, seg_ids, sinks)
    group_cols = HQ * HD // N_ROW
    hidden = tokens.astype(jnp.float32)
    for group_id in range(N_ROW):
        partial_value = jnp.dot(attended[:, group_id * group_cols:(group_id + 1) * group_cols], out_weight[group_id * group_cols:(group_id + 1) * group_cols], preferred_element_type=jnp.float32).astype(jnp.bfloat16)
        partial_value = lax.optimization_barrier(partial_value)
        hidden = hidden + partial_value.astype(jnp.float32)
    moe_in = rms_scale(hidden, moe_gain).astype(jnp.bfloat16)
    mixed = (hidden + experts_all(moe_in, routes, route_weights, expert_in, expert_out)).astype(jnp.bfloat16)
    return (mixed, kv_cache)
```

```python
import math

import jax
import jax.numpy as jnp
from jax import lax
from jax.experimental import pallas as pl
from jax.experimental.pallas import tpu as pltpu
from jax.sharding import PartitionSpec as P

HD = 64
WIN = 128
EXPERTS = 64
TOP = 4
CAP = 9


eps_norm = 1e-05
theta_base = 150000.0
glu_alpha = 1.702
masked_score = -1e30


def from_behind(value, axis, steps):
    count = lax.axis_size(axis)
    first, last = (max(0, -steps), min(count, count - steps))
    return lax.ppermute(value, axis, [(source, source + steps) for source in range(first, last)])


def rms_scale(values_in, gain_vec):
    widened = values_in.astype(jnp.float32)
    return (
        widened
        * lax.rsqrt(jnp.mean(widened * widened, axis=-1, keepdims=True) + eps_norm)
        * gain_vec
    )


def rotate(values_in, positions):
    half_dim = values_in.shape[-1] // 2
    frequency = jnp.exp(
        jnp.arange(half_dim, dtype=jnp.float32)
        * (-2.0 * math.log(theta_base) / values_in.shape[-1])
    )
    angles = positions.astype(jnp.float32)[:, None] * frequency[None, :]
    cosine = jnp.cos(angles)[:, None, :]
    sine = jnp.sin(angles)[:, None, :]
    first_half = values_in[..., :half_dim]
    second_half = values_in[..., half_dim:]
    return jnp.concatenate(
        [first_half * cosine - second_half * sine, second_half * cosine + first_half * sine],
        axis=-1,
    )


def attend_tile(
    query_tile, key_tile, value_tile, query_seg, key_seg, query_pos, key_pos, sink_grid
):
    scores = jnp.einsum(
        "qkgd,lkd->kgql", query_tile, key_tile, preferred_element_type=jnp.float32
    ) * query_tile.shape[-1] ** (-0.5)
    distance = query_pos[:, None] - key_pos[None, :]
    allowed = (
        (query_seg[:, None] == key_seg[None, :])
        & (distance >= 0)
        & (distance < WIN)
        & (key_pos[None, :] >= 0)
    )
    scores = jnp.where(allowed[None, None], scores, masked_score)
    sink_col = sink_grid[:, :, None]
    ceiling = jnp.maximum(jnp.max(scores, axis=-1), sink_col)
    expo = jnp.exp(scores - ceiling[..., None])
    denom = jnp.sum(expo, axis=-1) + jnp.exp(sink_col - ceiling)
    probs = (expo / denom[..., None]).astype(jnp.bfloat16)
    return jnp.einsum(
        "kgql,lkd->qkgd", probs, value_tile, preferred_element_type=jnp.float32
    ).astype(jnp.bfloat16)


LANES = 128
MAIN = CAP - 1
FULL_VMEM = 56 * 1024 * 1024


def up_to(count, multiple):
    return -(-count // multiple) * multiple


def swap_rows(value, distance):
    count = lax.axis_size("row")
    return lax.ppermute(value, "row", [(place, place ^ distance) for place in range(count)])


def whole_spec():
    return pl.BlockSpec(memory_space=pltpu.VMEM)


def dot32(left, right):
    return jnp.dot(left, right, preferred_element_type=jnp.float32)


def piece_widths(feature_dim):
    piece = up_to(-(-feature_dim // MAIN), LANES)
    return up_to(feature_dim, LANES), piece


def as_bf16(condition):
    return jnp.where(condition, 1.0, 0.0).astype(jnp.bfloat16)


def dispatch_kernel(parts, share, feature_dim, groups, *refs):
    count = len(parts)
    tokens_ref, gain_ref = refs[:2]
    code_refs = refs[2 : 2 + groups]
    part_refs = refs[2 + groups : 2 + groups + sum(parts)]
    hidden_ref = refs[2 + groups + sum(parts)]
    out_refs = refs[3 + groups + sum(parts) : 3 + 2 * groups + sum(parts)]
    normed_ref = refs[-1]
    at = 0
    sums = []
    for index in range(count):
        total = part_refs[at][...].astype(jnp.float32)
        for other in range(1, parts[index]):
            total = total + part_refs[at + other][...].astype(jnp.float32)
        at += parts[index]
        sums.append(total)
    width = sum(share)
    pieces = []
    for block in range(feature_dim // width):
        for index in range(count):
            pieces.append(sums[index][:, block * share[index] : (block + 1) * share[index]])
    hidden = tokens_ref[...].astype(jnp.float32) + jnp.concatenate(pieces, axis=1)
    hidden_ref[...] = hidden
    scale = lax.rsqrt(jnp.mean(hidden * hidden, axis=-1, keepdims=True) + eps_norm)
    main_width, piece = piece_widths(feature_dim)
    normed_ref[...] = jnp.zeros_like(normed_ref)
    normed_ref[:, :feature_dim] = (hidden * scale * gain_ref[...]).astype(jnp.bfloat16)
    for code_ref, out_ref in zip(code_refs, out_refs):
        codes = code_ref[...]
        slot = lax.broadcasted_iota(jnp.int32, codes.shape, 0) % MAIN
        out_ref[:, :main_width] = dot32(
            as_bf16(codes == slot), normed_ref[:, :main_width]
        ).astype(jnp.bfloat16)
        tail = jnp.zeros((codes.shape[0], piece), jnp.float32)
        for j in range(MAIN):
            tail = tail + dot32(
                as_bf16((codes == MAIN) & (slot == j)), normed_ref[:, j * piece : (j + 1) * piece]
            )
        out_ref[:, main_width:] = tail.astype(jnp.bfloat16)


def dispatch(tokens, gain, codes, parts, share):
    rows, feature_dim = tokens.shape
    main_width, piece = piece_widths(feature_dim)
    flat = [part for group in parts for part in group]
    groups = len(codes)
    return pl.pallas_call(
        lambda *refs: dispatch_kernel(
            tuple(len(group) for group in parts), share, feature_dim, groups, *refs
        ),
        out_shape=[jax.ShapeDtypeStruct((rows, feature_dim), jnp.float32)]
        + [
            jax.ShapeDtypeStruct((code.shape[0], main_width + piece), jnp.bfloat16)
            for code in codes
        ],
        in_specs=[whole_spec()] * (2 + groups + len(flat)),
        out_specs=[whole_spec()] * (1 + groups),
        scratch_shapes=[pltpu.VMEM((rows, MAIN * piece), jnp.bfloat16)],
        compiler_params=pltpu.CompilerParams(vmem_limit_bytes=FULL_VMEM),
    )(tokens, gain, *codes, *flat)


def expert_kernel(feature_dim, x_ref, gate_ref, up_ref, down_ref, y_ref, x_all, total):
    main_width, piece = piece_widths(feature_dim)
    main_rows = x_ref.shape[0]
    senders = main_rows // MAIN
    step = pl.program_id(0) * pl.num_programs(1) + pl.program_id(1)
    last = pl.num_programs(0) * pl.num_programs(1) - 1

    @pl.when(step == 0)
    def _():
        x_all[:main_rows, :main_width] = x_ref[:, :main_width]
        row = lax.broadcasted_iota(jnp.int32, (senders, main_rows), 0)
        col = lax.broadcasted_iota(jnp.int32, (senders, main_rows), 1)
        tail = x_ref[:, main_width:]
        for j in range(MAIN):
            x_all[main_rows:, j * piece : (j + 1) * piece] = dot32(
                as_bf16(col == row * MAIN + j), tail
            ).astype(jnp.bfloat16)

    x = x_all[:, :feature_dim]
    gate_part = dot32(x, gate_ref[0])
    up_part = dot32(x, up_ref[0])
    hidden_act = (gate_part * jax.nn.sigmoid(glu_alpha * gate_part) * (up_part + 1.0)).astype(
        jnp.bfloat16
    )
    product = lax.dot_general(
        hidden_act, down_ref[0], (((1,), (1,)), ((), ())), preferred_element_type=jnp.float32
    )

    @pl.when(step == 0)
    def _():
        total[...] = product

    @pl.when(step > 0)
    def _():
        total[...] += product

    @pl.when(step == last)
    def _():
        y_ref[:, feature_dim:main_width] = jnp.zeros(
            (main_rows, main_width - feature_dim), jnp.bfloat16
        )
        y_ref[:, :feature_dim] = total[:main_rows].astype(jnp.bfloat16)
        x_all[main_rows:, :] = jnp.zeros((senders, MAIN * piece), jnp.bfloat16)
        x_all[main_rows:, :feature_dim] = total[main_rows:].astype(jnp.bfloat16)
        row = lax.broadcasted_iota(jnp.int32, (main_rows, senders), 0)
        col = lax.broadcasted_iota(jnp.int32, (main_rows, senders), 1)
        tail = jnp.zeros((main_rows, piece), jnp.float32)
        for j in range(MAIN):
            tail = tail + dot32(
                as_bf16(row == col * MAIN + j), x_all[main_rows:, j * piece : (j + 1) * piece]
            )
        y_ref[:, main_width:] = tail.astype(jnp.bfloat16)


def experts(x, expert_in, expert_out, first, halves):
    feature_dim, hidden_width = expert_in.shape[1], expert_out.shape[1]
    main_width, piece = piece_widths(feature_dim)
    rows = x.shape[0] + x.shape[0] // MAIN
    block = math.gcd(hidden_width, 256 if rows <= 512 else 128)
    steps = hidden_width // block
    cost = 6 * rows * feature_dim * hidden_width * halves
    return pl.pallas_call(
        lambda *refs: expert_kernel(feature_dim, *refs),
        grid=(halves, steps),
        out_shape=jax.ShapeDtypeStruct(x.shape, jnp.bfloat16),
        in_specs=[
            pl.BlockSpec(x.shape, lambda j, f: (0, 0)),
            pl.BlockSpec((1, feature_dim, block), lambda j, f: (first + j, 0, f)),
            pl.BlockSpec((1, feature_dim, block), lambda j, f: (first + j, 0, steps + f)),
            pl.BlockSpec((1, feature_dim, block), lambda j, f: (first + j, 0, f)),
        ],
        out_specs=pl.BlockSpec(x.shape, lambda j, f: (0, 0)),
        scratch_shapes=[
            pltpu.VMEM((rows, MAIN * piece), jnp.bfloat16),
            pltpu.VMEM((rows, feature_dim), jnp.float32),
        ],
        compiler_params=pltpu.CompilerParams(
            vmem_limit_bytes=FULL_VMEM, dimension_semantics=("arbitrary", "arbitrary")
        ),
        cost_estimate=pl.CostEstimate(
            flops=cost,
            bytes_accessed=6 * feature_dim * hidden_width * halves,
            transcendentals=rows * hidden_width * halves,
        ),
    )(x, expert_in, expert_in, jnp.swapaxes(expert_out, 1, 2))


def combine_kernel(turned, hidden_ref, back_ref, code_ref, weight_ref, out_ref):
    feature_dim = hidden_ref.shape[1]
    main_width, piece = piece_widths(feature_dim)
    codes = code_ref[...]
    slot = lax.broadcasted_iota(jnp.int32, codes.shape, 1) % MAIN
    weights = weight_ref[...]
    high = weights.astype(jnp.bfloat16).astype(jnp.float32)
    low = weights - high

    def pick(condition):
        return [
            jnp.where(condition, part, 0.0).astype(jnp.bfloat16) for part in (high, low)
        ]

    tail = back_ref[:, main_width:]
    main = pick(codes == slot)
    for j in range(MAIN):
        first, end = j * piece, min((j + 1) * piece, feature_dim)
        ninth = pick((codes == MAIN) & (slot == j))
        value = hidden_ref[:, first:end]
        for k in range(2):
            value = value + dot32(main[k], back_ref[:, first:end])
            value = value + dot32(ninth[k], tail)[:, : end - first]
        if turned:
            out_ref[first:end, :] = value.T.astype(out_ref.dtype)
        else:
            out_ref[:, first:end] = value


def combine(hidden, back, codes, weights, turned):
    rows, feature_dim = hidden.shape
    return pl.pallas_call(
        lambda *refs: combine_kernel(turned, *refs),
        out_shape=jax.ShapeDtypeStruct((feature_dim, rows), jnp.bfloat16)
        if turned
        else jax.ShapeDtypeStruct((rows, feature_dim), jnp.float32),
        in_specs=[whole_spec()] * 4,
        out_specs=whole_spec(),
        compiler_params=pltpu.CompilerParams(vmem_limit_bytes=FULL_VMEM),
    )(hidden, back, codes, weights)


def shards(
    tokens,
    seg_ids,
    norm_gain,
    query_weight,
    kv_weight,
    out_weight,
    sinks,
    moe_gain,
    routes,
    route_weights,
    expert_in,
    expert_out,
):
    own_rows, feature_dim = tokens.shape
    row_count, col_count = lax.axis_size("row"), lax.axis_size("col")
    device_count = row_count * col_count
    row_at, col_at = lax.axis_index("row"), lax.axis_index("col")
    query_cols, kv_cols = query_weight.shape[1], kv_weight.shape[1]

    proj_weight = lax.all_gather(
        jnp.concatenate([query_weight, kv_weight], axis=1), "col", axis=0, tiled=True
    )
    out_cols = out_weight.shape[1]
    cut = up_to(2 * out_cols // 3, 8)
    out_parts = [
        lax.all_gather(part, "col", axis=1, tiled=True)
        for part in (out_weight[:, :cut], out_weight[:, cut:])
    ]

    normed = rms_scale(tokens, norm_gain).astype(jnp.bfloat16)
    block_x = jnp.zeros((row_count, own_rows, feature_dim), jnp.bfloat16)
    for distance in range(row_count):
        piece = swap_rows(normed, distance) if distance else normed
        block_x = lax.dynamic_update_index_in_dim(block_x, piece, row_at ^ distance, 0)
    block_rows = row_count * own_rows
    block_x = block_x.reshape(block_rows, feature_dim)

    all_segs = lax.all_to_all(
        jnp.broadcast_to(seg_ids[None, :], (device_count, own_rows)),
        ("col", "row"),
        split_axis=0,
        concat_axis=0,
        tiled=True,
    ).reshape(-1)
    base_index = col_at * block_rows
    padded_segs = jnp.concatenate([jnp.full((WIN,), -1, jnp.int32), all_segs])
    key_seg = lax.dynamic_slice_in_dim(padded_segs, base_index, WIN + block_rows, 0)
    block_seg = key_seg[WIN:]
    token_index = base_index + jnp.arange(block_rows, dtype=jnp.int32)
    starts = jnp.sum((all_segs[None, :] < block_seg[:, None]).astype(jnp.int32), axis=1)
    positions = token_index - starts

    slices_here = expert_in.shape[0]
    groups = max(1, slices_here // 2)
    halves = min(2, slices_here)
    expert_ids = jnp.arange(EXPERTS, dtype=jnp.int32)
    named = routes[:, :, None] == expert_ids[None, None, :]
    hits = jnp.sum(named.astype(jnp.float32), axis=1)
    expert_weight = jnp.sum(jnp.where(named, route_weights[:, :, None], 0.0), axis=1)
    ranks = jnp.cumsum(hits, axis=0) - hits
    ranks = jnp.where(hits > 0, ranks, -1.0).astype(jnp.int32)
    code_in, code_out, weight_out = [], [], []
    for group in range(groups):
        chosen = jnp.arange(device_count, dtype=jnp.int32) * slices_here // 2 + group
        spread = jnp.repeat(ranks[:, chosen], MAIN, axis=1)
        code_out.append(spread)
        code_in.append(spread.T)
        weight_out.append(jnp.repeat(expert_weight[:, chosen], MAIN, axis=1))

    proj_sum = dot32(block_x, proj_weight)
    query_sum, kv_sum = proj_sum[:, :query_cols], proj_sum[:, query_cols:]
    query_heads = query_cols // HD
    kv_heads = kv_cols // (2 * HD)
    group_size = query_heads // kv_heads
    queries = rotate(query_sum.reshape(block_rows, query_heads, HD), positions).astype(jnp.bfloat16)
    kv_pair = kv_sum.reshape(block_rows, kv_heads, 2, HD)
    keys = rotate(kv_pair[:, :, 0], positions).astype(jnp.bfloat16)
    values = kv_pair[:, :, 1].astype(jnp.bfloat16)
    kv_cache = jnp.stack([keys, values], axis=2).reshape(block_rows, kv_cols)
    edge_kv = from_behind(kv_cache[block_rows - WIN :], "col", 1)
    all_kv = jnp.concatenate([edge_kv, kv_cache], axis=0).reshape(WIN + block_rows, kv_heads, 2, HD)
    key_index = base_index - WIN + jnp.arange(WIN + block_rows, dtype=jnp.int32)
    query_grid = queries.reshape(block_rows, kv_heads, group_size, HD)
    sink_grid = sinks.reshape(kv_heads, group_size)
    attended = attend_tile(
        query_grid,
        all_kv[:, :, 0],
        all_kv[:, :, 1],
        block_seg,
        key_seg,
        token_index,
        key_index,
        sink_grid,
    ).reshape(block_rows, query_cols)

    sums = []
    for part in out_parts:
        if sums:
            part, sums = lax.optimization_barrier((part, sums))
        partial = dot32(attended, part).astype(jnp.bfloat16)
        partial = partial.reshape(row_count, own_rows, part.shape[1])
        pieces = []
        for distance in range(row_count):
            piece = lax.dynamic_index_in_dim(partial, row_at ^ distance, 0, False)
            pieces.append(swap_rows(piece, distance) if distance else piece)
        sums.append(pieces)

    hidden, *outgoing = dispatch(
        tokens, moe_gain.reshape(1, feature_dim), code_in, sums, (cut, out_cols - cut)
    )
    for group in range(groups):
        shape = (device_count, MAIN, outgoing[group].shape[1])
        arrived = lax.all_to_all(
            outgoing[group].reshape(shape), ("row", "col"), split_axis=0, concat_axis=0, tiled=True
        )
        produced = experts(
            arrived.reshape(outgoing[group].shape), expert_in, expert_out, group * halves, halves
        )
        returned = lax.all_to_all(
            produced.reshape(shape), ("row", "col"), split_axis=0, concat_axis=0, tiled=True
        )
        hidden = combine(
            hidden,
            returned.reshape(outgoing[group].shape),
            code_out[group],
            weight_out[group],
            group == groups - 1,
        )
    return (hidden.T, kv_cache)


def solution(mesh):
    in_specs = (
        P(("col", "row"), None),
        P(("col", "row")),
        P(),
        P("col", "row"),
        P("col", "row"),
        P("row", "col"),
        P("row"),
        P(),
        P(("col", "row"), None),
        P(("col", "row"), None),
        P(("row", "col"), None, None),
        P(("row", "col"), None, None),
    )
    out_specs = (P(("col", "row"), None), P("col", "row"))
    return jax.shard_map(shards, mesh=mesh, in_specs=in_specs, out_specs=out_specs, check_vma=False)
```

```python
import math

import jax
import jax.numpy as jnp
from jax import lax
from jax.experimental import pallas as pl
from jax.experimental.pallas import tpu as pltpu
from jax.sharding import PartitionSpec as P

HD = 64
WIN = 128
EXPERTS = 64
TOP = 4
CAP = 9


eps_norm = 1e-05
theta_base = 150000.0
glu_alpha = 1.702
masked_score = -1e30


def from_behind(value, axis, steps):
    count = lax.axis_size(axis)
    first, last = (max(0, -steps), min(count, count - steps))
    return lax.ppermute(value, axis, [(source, source + steps) for source in range(first, last)])


def rms_scale(values_in, gain_vec):
    widened = values_in.astype(jnp.float32)
    return (
        widened
        * lax.rsqrt(jnp.mean(widened * widened, axis=-1, keepdims=True) + eps_norm)
        * gain_vec
    )


def rotate(values_in, positions):
    half_dim = values_in.shape[-1] // 2
    frequency = jnp.exp(
        jnp.arange(half_dim, dtype=jnp.float32)
        * (-2.0 * math.log(theta_base) / values_in.shape[-1])
    )
    angles = positions.astype(jnp.float32)[:, None] * frequency[None, :]
    cosine = jnp.cos(angles)[:, None, :]
    sine = jnp.sin(angles)[:, None, :]
    first_half = values_in[..., :half_dim]
    second_half = values_in[..., half_dim:]
    return jnp.concatenate(
        [first_half * cosine - second_half * sine, second_half * cosine + first_half * sine],
        axis=-1,
    )


def attend_tile(
    query_tile, key_tile, value_tile, query_seg, key_seg, query_pos, key_pos, sink_grid
):
    scores = jnp.einsum(
        "qkgd,lkd->kgql", query_tile, key_tile, preferred_element_type=jnp.float32
    ) * query_tile.shape[-1] ** (-0.5)
    distance = query_pos[:, None] - key_pos[None, :]
    allowed = (
        (query_seg[:, None] == key_seg[None, :])
        & (distance >= 0)
        & (distance < WIN)
        & (key_pos[None, :] >= 0)
    )
    scores = jnp.where(allowed[None, None], scores, masked_score)
    sink_col = sink_grid[:, :, None]
    ceiling = jnp.maximum(jnp.max(scores, axis=-1), sink_col)
    expo = jnp.exp(scores - ceiling[..., None])
    denom = jnp.sum(expo, axis=-1) + jnp.exp(sink_col - ceiling)
    probs = (expo / denom[..., None]).astype(jnp.bfloat16)
    return jnp.einsum(
        "kgql,lkd->qkgd", probs, value_tile, preferred_element_type=jnp.float32
    ).astype(jnp.bfloat16)


LANES = 128
MAIN = CAP - 1
FULL_VMEM = 56 * 1024 * 1024


def up_to(count, multiple):
    return -(-count // multiple) * multiple


def swap_rows(value, distance):
    count = lax.axis_size("row")
    return lax.ppermute(value, "row", [(place, place ^ distance) for place in range(count)])


def gather_by_permutes(block):
    count = lax.axis_size("col")
    place = lax.axis_index("col")
    chips, size = count // 2, block.shape[0]
    line = []
    for distance in reversed(range(chips)):
        piece = block
        if distance:
            pairs = [(at, (at + 2 * distance) % count) for at in range(count)]
            piece = lax.ppermute(block, "col", pairs)
        line.append(piece)
    line = jnp.concatenate(line, axis=0).reshape(chips, size, -1)
    across = lax.ppermute(line, "col", [(at, at ^ 1) for at in range(count)])
    even = place % 2 == 0
    line = jnp.stack([jnp.where(even, line, across), jnp.where(even, across, line)], axis=1)
    line = line.reshape(count * size, -1)
    start = (2 * chips - 1 - place // 2) % chips * 2 * size
    return lax.dynamic_slice_in_dim(jnp.concatenate([line, line], axis=0), start, count * size, 0)


def project_kernel(x_ref, weight_ref, out_ref):
    out_ref[...] = dot32(x_ref[...], weight_ref[...])


def project(x, weight):
    rows, depth = x.shape
    columns = weight.shape[1]
    block = math.gcd(columns, 256)
    return pl.pallas_call(
        project_kernel,
        grid=(columns // block,),
        out_shape=jax.ShapeDtypeStruct((rows, columns), jnp.float32),
        in_specs=[
            pl.BlockSpec((rows, depth), lambda at: (0, 0)),
            pl.BlockSpec((depth, block), lambda at: (0, at)),
        ],
        out_specs=pl.BlockSpec((rows, block), lambda at: (0, at)),
        compiler_params=pltpu.CompilerParams(
            vmem_limit_bytes=FULL_VMEM, dimension_semantics=("arbitrary",)
        ),
        cost_estimate=pl.CostEstimate(
            flops=2 * rows * depth * columns,
            bytes_accessed=2 * depth * (rows + columns) + 4 * rows * columns,
            transcendentals=0,
        ),
    )(x, weight)


def whole_spec():
    return pl.BlockSpec(memory_space=pltpu.VMEM)


def dot32(left, right):
    return jnp.dot(left, right, preferred_element_type=jnp.float32)


def piece_widths(feature_dim):
    piece = up_to(-(-feature_dim // MAIN), LANES)
    return up_to(feature_dim, LANES), piece


def as_bf16(condition):
    return jnp.where(condition, 1.0, 0.0).astype(jnp.bfloat16)


def hidden_kernel(counts, share, *refs):
    tokens_ref, gain_ref = refs[:2]
    part_refs, (hidden_ref, normed_ref) = refs[2:-2], refs[-2:]
    at = 0
    sums = []
    for count in counts:
        total = part_refs[at][...].astype(jnp.float32)
        for other in range(1, count):
            total = total + part_refs[at + other][...].astype(jnp.float32)
        at += count
        sums.append(total)
    pieces = []
    for block in range(tokens_ref.shape[1] // sum(share)):
        for size, total in zip(share, sums):
            pieces.append(total[:, block * size : (block + 1) * size])
    hidden = tokens_ref[...].astype(jnp.float32) + jnp.concatenate(pieces, axis=1)
    hidden_ref[...] = hidden
    scale = lax.rsqrt(jnp.mean(hidden * hidden, axis=-1, keepdims=True) + eps_norm)
    normed_ref[...] = (hidden * scale * gain_ref[...]).astype(jnp.bfloat16)


def hidden_and_norm(tokens, gain, parts, share):
    flat = [part for group in parts for part in group]
    return pl.pallas_call(
        lambda *refs: hidden_kernel(tuple(len(group) for group in parts), share, *refs),
        out_shape=[
            jax.ShapeDtypeStruct(tokens.shape, jnp.float32),
            jax.ShapeDtypeStruct(tokens.shape, jnp.bfloat16),
        ],
        in_specs=[whole_spec()] * (2 + len(flat)),
        out_specs=[whole_spec()] * 2,
        compiler_params=pltpu.CompilerParams(vmem_limit_bytes=FULL_VMEM),
    )(tokens, gain, *flat)


def pack_kernel(rows_ref, code_ref, out_ref, padded_ref):
    feature_dim = rows_ref.shape[1]
    main_width, piece = piece_widths(feature_dim)
    padded_ref[...] = jnp.zeros_like(padded_ref)
    padded_ref[:, :feature_dim] = rows_ref[...]
    for group in range(code_ref.shape[0]):
        codes = code_ref[group]
        slot = lax.broadcasted_iota(jnp.int32, codes.shape, 0) % MAIN
        fold = (codes.shape[0] // MAIN, MAIN, -1)
        out_ref[:, group, :, :main_width] = (
            dot32(as_bf16(codes == slot), padded_ref[:, :main_width])
            .reshape(fold)
            .astype(jnp.bfloat16)
        )
        tail = jnp.zeros((codes.shape[0], piece), jnp.float32)
        for j in range(MAIN):
            tail = tail + dot32(
                as_bf16((codes == MAIN) & (slot == j)), padded_ref[:, j * piece : (j + 1) * piece]
            )
        out_ref[:, group, :, main_width:] = tail.reshape(fold).astype(jnp.bfloat16)


def pack(rows, codes):
    main_width, piece = piece_widths(rows.shape[1])
    return pl.pallas_call(
        pack_kernel,
        out_shape=jax.ShapeDtypeStruct(
            (codes.shape[1] // MAIN, codes.shape[0], MAIN, main_width + piece), jnp.bfloat16
        ),
        in_specs=[whole_spec()] * 2,
        out_specs=whole_spec(),
        scratch_shapes=[pltpu.VMEM((rows.shape[0], MAIN * piece), jnp.bfloat16)],
        compiler_params=pltpu.CompilerParams(vmem_limit_bytes=FULL_VMEM),
    )(rows, codes)


def expert_kernel(feature_dim, x_ref, gate_ref, up_ref, down_ref, y_ref, x_all, total):
    main_width, piece = piece_widths(feature_dim)
    senders = x_ref.shape[0]
    main_rows = senders * MAIN
    step = pl.program_id(1) * pl.num_programs(2) + pl.program_id(2)
    last = pl.num_programs(1) * pl.num_programs(2) - 1

    @pl.when(step == 0)
    def _():
        x_all[:main_rows, :main_width] = x_ref[:, 0, :, :main_width].reshape(main_rows, main_width)
        row = lax.broadcasted_iota(jnp.int32, (senders, main_rows), 0)
        col = lax.broadcasted_iota(jnp.int32, (senders, main_rows), 1)
        tail = x_ref[:, 0, :, main_width:].reshape(main_rows, piece)
        for j in range(MAIN):
            x_all[main_rows:, j * piece : (j + 1) * piece] = dot32(
                as_bf16(col == row * MAIN + j), tail
            ).astype(jnp.bfloat16)

    x = x_all[:, :feature_dim]
    gate_part = dot32(x, gate_ref[0])
    up_part = dot32(x, up_ref[0])
    hidden_act = (gate_part * jax.nn.sigmoid(glu_alpha * gate_part) * (up_part + 1.0)).astype(
        jnp.bfloat16
    )
    product = lax.dot_general(
        hidden_act, down_ref[0], (((1,), (1,)), ((), ())), preferred_element_type=jnp.float32
    )

    @pl.when(step == 0)
    def _():
        total[...] = product

    @pl.when(step > 0)
    def _():
        total[...] += product

    @pl.when(step == last)
    def _():
        y_ref[:, 0, :, feature_dim:main_width] = jnp.zeros(
            (senders, MAIN, main_width - feature_dim), jnp.bfloat16
        )
        y_ref[:, 0, :, :feature_dim] = (
            total[:main_rows].reshape(senders, MAIN, feature_dim).astype(jnp.bfloat16)
        )
        x_all[main_rows:, :] = jnp.zeros((senders, MAIN * piece), jnp.bfloat16)
        x_all[main_rows:, :feature_dim] = total[main_rows:].astype(jnp.bfloat16)
        row = lax.broadcasted_iota(jnp.int32, (main_rows, senders), 0)
        col = lax.broadcasted_iota(jnp.int32, (main_rows, senders), 1)
        tail = jnp.zeros((main_rows, piece), jnp.float32)
        for j in range(MAIN):
            tail = tail + dot32(
                as_bf16(row == col * MAIN + j), x_all[main_rows:, j * piece : (j + 1) * piece]
            )
        y_ref[:, 0, :, main_width:] = tail.reshape(senders, MAIN, piece).astype(jnp.bfloat16)


def experts(x, expert_in, expert_out, halves):
    senders, groups, _, width = x.shape
    main_rows = senders * MAIN
    feature_dim, hidden_width = expert_in.shape[1], expert_out.shape[1]
    main_width, piece = piece_widths(feature_dim)
    rows = main_rows + main_rows // MAIN
    block = math.gcd(hidden_width, 768 if rows <= 512 else 128)
    steps = hidden_width // block
    slices = groups * halves
    return pl.pallas_call(
        lambda *refs: expert_kernel(feature_dim, *refs),
        grid=(groups, halves, steps),
        out_shape=jax.ShapeDtypeStruct(x.shape, jnp.bfloat16),
        in_specs=[
            pl.BlockSpec((senders, 1, MAIN, width), lambda g, j, f: (0, g, 0, 0)),
            pl.BlockSpec((1, feature_dim, block), lambda g, j, f: (g * halves + j, 0, f)),
            pl.BlockSpec((1, feature_dim, block), lambda g, j, f: (g * halves + j, 0, steps + f)),
            pl.BlockSpec((1, feature_dim, block), lambda g, j, f: (g * halves + j, 0, f)),
        ],
        out_specs=pl.BlockSpec((senders, 1, MAIN, width), lambda g, j, f: (0, g, 0, 0)),
        scratch_shapes=[
            pltpu.VMEM((rows, MAIN * piece), jnp.bfloat16),
            pltpu.VMEM((rows, feature_dim), jnp.float32),
        ],
        compiler_params=pltpu.CompilerParams(
            vmem_limit_bytes=FULL_VMEM, dimension_semantics=("arbitrary",) * 3
        ),
        cost_estimate=pl.CostEstimate(
            flops=6 * rows * feature_dim * hidden_width * slices,
            bytes_accessed=6 * feature_dim * hidden_width * slices,
            transcendentals=rows * hidden_width * slices,
        ),
    )(x, expert_in, expert_in, jnp.swapaxes(expert_out, 1, 2))


def combine_kernel(start_ref, back_ref, code_ref, weight_ref, out_ref):
    feature_dim = out_ref.shape[1]
    main_width, piece = piece_widths(feature_dim)
    senders, groups = back_ref.shape[:2]
    rows = senders * MAIN
    picks = []
    for group in range(groups):
        codes = code_ref[group]
        slot = lax.broadcasted_iota(jnp.int32, codes.shape, 1) % MAIN
        weights = weight_ref[group]
        high = weights.astype(jnp.bfloat16).astype(jnp.float32)
        picks.append((codes, slot, (high, weights - high)))

    def pick(group, chosen):
        codes, slot, parts = picks[group]
        condition = (codes == slot) if chosen is None else (codes == MAIN) & (slot == chosen)
        return [jnp.where(condition, part, 0.0).astype(jnp.bfloat16) for part in parts]

    main = [pick(group, None) for group in range(groups)]
    for j in range(MAIN):
        first, end = j * piece, min((j + 1) * piece, feature_dim)
        value = 0.0 if start_ref is None else start_ref[:, first:end]
        for group in range(groups):
            ninth = pick(group, j)
            tail = back_ref[:, group, :, main_width : main_width + end - first].reshape(rows, -1)
            part = back_ref[:, group, :, first:end].reshape(rows, -1)
            for k in range(2):
                value = value + dot32(main[group][k], part)
                value = value + dot32(ninth[k], tail)
        out_ref[:, first:end] = value.astype(out_ref.dtype)


def combine(start, back, codes, weights, feature_dim):
    alone = start is None
    given = (back, codes, weights) if alone else (start, back, codes, weights)
    return pl.pallas_call(
        (lambda *refs: combine_kernel(None, *refs)) if alone else combine_kernel,
        out_shape=jax.ShapeDtypeStruct(
            (codes.shape[1], feature_dim), jnp.bfloat16 if alone else jnp.float32
        ),
        in_specs=[whole_spec()] * len(given),
        out_specs=whole_spec(),
        compiler_params=pltpu.CompilerParams(vmem_limit_bytes=FULL_VMEM),
    )(*given)


def final_kernel(near_ref, far_ref, out_ref):
    out_ref[...] = (near_ref[...] + far_ref[...].astype(jnp.float32)).T.astype(out_ref.dtype)


def final_sum(near, far):
    rows, feature_dim = near.shape
    return pl.pallas_call(
        final_kernel,
        out_shape=jax.ShapeDtypeStruct((feature_dim, rows), jnp.bfloat16),
        in_specs=[whole_spec()] * 2,
        out_specs=whole_spec(),
        compiler_params=pltpu.CompilerParams(vmem_limit_bytes=FULL_VMEM),
    )(near, far).T


def mirrored(value):
    count = lax.axis_size("col")
    return lax.ppermute(value, "col", [(at, (at + count // 2) % count) for at in range(count)])


def exchange(value):
    rows, cols = lax.axis_size("row"), lax.axis_size("col")
    near = cols // 2
    halves = [
        [row * cols + side * near + at for row in range(rows) for at in range(near)]
        for side in (0, 1)
    ]
    return lax.all_to_all(
        value, ("row", "col"), split_axis=0, concat_axis=0, axis_index_groups=halves, tiled=True
    )


def shards(
    tokens,
    seg_ids,
    norm_gain,
    query_weight,
    kv_weight,
    out_weight,
    sinks,
    moe_gain,
    routes,
    route_weights,
    expert_in,
    expert_out,
):
    own_rows, feature_dim = tokens.shape
    row_count, col_count = lax.axis_size("row"), lax.axis_size("col")
    device_count = row_count * col_count
    row_at, col_at = lax.axis_index("row"), lax.axis_index("col")
    query_cols, kv_cols = query_weight.shape[1], kv_weight.shape[1]

    all_query = lax.all_gather(query_weight, "col", axis=0, tiled=True)
    all_kv_weight = gather_by_permutes(kv_weight)
    out_cols = out_weight.shape[1]
    cut = up_to(2 * out_cols // 3, 8)
    out_parts = [
        lax.all_gather(part, "col", axis=1, tiled=True)
        for part in (out_weight[:, :cut], out_weight[:, cut:])
    ]

    normed = rms_scale(tokens, norm_gain).astype(jnp.bfloat16)
    block_x = jnp.zeros((row_count, own_rows, feature_dim), jnp.bfloat16)
    for distance in range(row_count):
        piece = swap_rows(normed, distance) if distance else normed
        block_x = lax.dynamic_update_index_in_dim(block_x, piece, row_at ^ distance, 0)
    block_rows = row_count * own_rows
    block_x = block_x.reshape(block_rows, feature_dim)

    all_segs = lax.all_to_all(
        jnp.broadcast_to(seg_ids[None, :], (device_count, own_rows)),
        ("col", "row"),
        split_axis=0,
        concat_axis=0,
        tiled=True,
    ).reshape(-1)
    base_index = col_at * block_rows
    padded_segs = jnp.concatenate([jnp.full((WIN,), -1, jnp.int32), all_segs])
    key_seg = lax.dynamic_slice_in_dim(padded_segs, base_index, WIN + block_rows, 0)
    block_seg = key_seg[WIN:]
    token_index = base_index + jnp.arange(block_rows, dtype=jnp.int32)
    starts = jnp.sum((all_segs[None, :] < block_seg[:, None]).astype(jnp.int32), axis=1)
    positions = token_index - starts

    slices_here = expert_in.shape[0]
    groups = max(1, slices_here // 2)
    halves = min(2, slices_here)
    near_cols = col_count // 2
    members = jnp.arange(row_count * near_cols, dtype=jnp.int32)
    member_at = (
        members // near_cols * col_count + members % near_cols + col_at // near_cols * near_cols
    )

    def slots(route_ids, weights_in):
        expert_ids = jnp.arange(EXPERTS, dtype=jnp.int32)
        named = route_ids[:, :, None] == expert_ids[None, None, :]
        hits = jnp.sum(named.astype(jnp.float32), axis=1)
        expert_weight = jnp.sum(jnp.where(named, weights_in[:, :, None], 0.0), axis=1)
        ranks = jnp.cumsum(hits, axis=0) - hits
        ranks = jnp.where(hits > 0, ranks, -1.0).astype(jnp.int32)
        code_in, code_out, weight_out = [], [], []
        for group in range(groups):
            chosen = member_at * slices_here // 2 + group
            spread = jnp.repeat(ranks[:, chosen], MAIN, axis=1)
            code_out.append(spread)
            code_in.append(spread.T)
            weight_out.append(jnp.repeat(expert_weight[:, chosen], MAIN, axis=1))
        return jnp.stack(code_in), jnp.stack(code_out), jnp.stack(weight_out)

    own_in, own_out, own_weight = slots(routes, route_weights)
    far_in, far_out, far_weight = slots(mirrored(routes), mirrored(route_weights))

    all_query, all_kv_weight, *codes = lax.optimization_barrier(
        (all_query, all_kv_weight, own_in, own_out, own_weight, far_in, far_out, far_weight)
    )
    own_in, own_out, own_weight, far_in, far_out, far_weight = codes
    kv_sum = project(block_x, all_kv_weight)
    query_sum = project(block_x, all_query)
    query_heads = query_cols // HD
    kv_heads = kv_cols // (2 * HD)
    group_size = query_heads // kv_heads
    queries = rotate(query_sum.reshape(block_rows, query_heads, HD), positions).astype(jnp.bfloat16)
    kv_pair = kv_sum.reshape(block_rows, kv_heads, 2, HD)
    keys = rotate(kv_pair[:, :, 0], positions).astype(jnp.bfloat16)
    values = kv_pair[:, :, 1].astype(jnp.bfloat16)
    kv_cache = jnp.stack([keys, values], axis=2).reshape(block_rows, kv_cols)
    edge_kv = from_behind(kv_cache[block_rows - WIN :], "col", 1)
    all_kv = jnp.concatenate([edge_kv, kv_cache], axis=0).reshape(WIN + block_rows, kv_heads, 2, HD)
    key_index = base_index - WIN + jnp.arange(WIN + block_rows, dtype=jnp.int32)
    query_grid = queries.reshape(block_rows, kv_heads, group_size, HD)
    sink_grid = sinks.reshape(kv_heads, group_size)
    attended = attend_tile(
        query_grid,
        all_kv[:, :, 0],
        all_kv[:, :, 1],
        block_seg,
        key_seg,
        token_index,
        key_index,
        sink_grid,
    ).reshape(block_rows, query_cols)

    sums = []
    for part in out_parts:
        if sums:
            part, sums = lax.optimization_barrier((part, sums))
        partial = dot32(attended, part).astype(jnp.bfloat16)
        partial = partial.reshape(row_count, own_rows, part.shape[1])
        pieces = []
        for distance in range(row_count):
            piece = lax.dynamic_index_in_dim(partial, row_at ^ distance, 0, False)
            pieces.append(swap_rows(piece, distance) if distance else piece)
        sums.append(pieces)

    hidden, moe_in = hidden_and_norm(
        tokens, moe_gain.reshape(1, feature_dim), sums, (cut, out_cols - cut)
    )
    far_rows = mirrored(moe_in)
    own_came = exchange(pack(moe_in, own_in))
    far_rows, own_came = lax.optimization_barrier((far_rows, own_came))
    far_came = exchange(pack(far_rows, far_in))
    own_made = experts(own_came, expert_in, expert_out, halves)
    far_came, own_made = lax.optimization_barrier((far_came, own_made))
    own_back = exchange(own_made)
    far_made = experts(far_came, expert_in, expert_out, halves)
    far_made, own_back = lax.optimization_barrier((far_made, own_back))
    far_back = exchange(far_made)
    near_sum = combine(hidden, own_back, own_out, own_weight, feature_dim)
    far_sum = mirrored(combine(None, far_back, far_out, far_weight, feature_dim))
    return (final_sum(near_sum, far_sum), kv_cache)


def solution(mesh):
    in_specs = (
        P(("col", "row"), None),
        P(("col", "row")),
        P(),
        P("col", "row"),
        P("col", "row"),
        P("row", "col"),
        P("row"),
        P(),
        P(("col", "row"), None),
        P(("col", "row"), None),
        P(("row", "col"), None, None),
        P(("row", "col"), None, None),
    )
    out_specs = (P(("col", "row"), None), P("col", "row"))
    return jax.shard_map(shards, mesh=mesh, in_specs=in_specs, out_specs=out_specs, check_vma=False)
```

```python
import math

import jax
import jax.numpy as jnp
from jax import lax
from jax.experimental import pallas as pl
from jax.experimental.pallas import tpu as pltpu
from jax.sharding import PartitionSpec as P

HD = 64
WIN = 128
EXPERTS = 64
TOP = 4
CAP = 9


eps_norm = 1e-05
theta_base = 150000.0
glu_alpha = 1.702
masked_score = -1e30


def from_behind(value, axis, steps):
    count = lax.axis_size(axis)
    first, last = (max(0, -steps), min(count, count - steps))
    return lax.ppermute(value, axis, [(source, source + steps) for source in range(first, last)])


def rms_scale(values_in, gain_vec):
    widened = values_in.astype(jnp.float32)
    return (
        widened
        * lax.rsqrt(jnp.mean(widened * widened, axis=-1, keepdims=True) + eps_norm)
        * gain_vec
    )


def rotate(values_in, positions):
    half_dim = values_in.shape[-1] // 2
    frequency = jnp.exp(
        jnp.arange(half_dim, dtype=jnp.float32)
        * (-2.0 * math.log(theta_base) / values_in.shape[-1])
    )
    angles = positions.astype(jnp.float32)[:, None] * frequency[None, :]
    cosine = jnp.cos(angles)[:, None, :]
    sine = jnp.sin(angles)[:, None, :]
    first_half = values_in[..., :half_dim]
    second_half = values_in[..., half_dim:]
    return jnp.concatenate(
        [first_half * cosine - second_half * sine, second_half * cosine + first_half * sine],
        axis=-1,
    )


def attend_tile(
    query_tile, key_tile, value_tile, query_seg, key_seg, query_pos, key_pos, sink_grid
):
    scores = jnp.einsum(
        "qkgd,lkd->kgql", query_tile, key_tile, preferred_element_type=jnp.float32
    ) * query_tile.shape[-1] ** (-0.5)
    distance = query_pos[:, None] - key_pos[None, :]
    allowed = (
        (query_seg[:, None] == key_seg[None, :])
        & (distance >= 0)
        & (distance < WIN)
        & (key_pos[None, :] >= 0)
    )
    scores = jnp.where(allowed[None, None], scores, masked_score)
    sink_col = sink_grid[:, :, None]
    ceiling = jnp.maximum(jnp.max(scores, axis=-1), sink_col)
    expo = jnp.exp(scores - ceiling[..., None])
    denom = jnp.sum(expo, axis=-1) + jnp.exp(sink_col - ceiling)
    probs = (expo / denom[..., None]).astype(jnp.bfloat16)
    return jnp.einsum(
        "kgql,lkd->qkgd", probs, value_tile, preferred_element_type=jnp.float32
    ).astype(jnp.bfloat16)


LANES = 128
MAIN = CAP - 1
FULL_VMEM = 56 * 1024 * 1024


def up_to(count, multiple):
    return -(-count // multiple) * multiple


def swap_rows(value, distance):
    count = lax.axis_size("row")
    return lax.ppermute(value, "row", [(place, place ^ distance) for place in range(count)])


def whole_spec():
    return pl.BlockSpec(memory_space=pltpu.VMEM)


def dot32(left, right):
    return jnp.dot(left, right, preferred_element_type=jnp.float32)


def piece_widths(feature_dim):
    piece = up_to(-(-feature_dim // MAIN), LANES)
    return up_to(feature_dim, LANES), piece


def as_bf16(condition):
    return jnp.where(condition, 1.0, 0.0).astype(jnp.bfloat16)


def hidden_kernel(counts, share, *refs):
    tokens_ref, gain_ref = refs[:2]
    part_refs, (hidden_ref, normed_ref) = refs[2:-2], refs[-2:]
    at = 0
    sums = []
    for count in counts:
        total = part_refs[at][...].astype(jnp.float32)
        for other in range(1, count):
            total = total + part_refs[at + other][...].astype(jnp.float32)
        at += count
        sums.append(total)
    pieces = []
    for block in range(tokens_ref.shape[1] // sum(share)):
        for size, total in zip(share, sums):
            pieces.append(total[:, block * size : (block + 1) * size])
    hidden = tokens_ref[...].astype(jnp.float32) + jnp.concatenate(pieces, axis=1)
    hidden_ref[...] = hidden
    scale = lax.rsqrt(jnp.mean(hidden * hidden, axis=-1, keepdims=True) + eps_norm)
    normed_ref[...] = (hidden * scale * gain_ref[...]).astype(jnp.bfloat16)


def hidden_and_norm(tokens, gain, parts, share):
    flat = [part for group in parts for part in group]
    return pl.pallas_call(
        lambda *refs: hidden_kernel(tuple(len(group) for group in parts), share, *refs),
        out_shape=[
            jax.ShapeDtypeStruct(tokens.shape, jnp.float32),
            jax.ShapeDtypeStruct(tokens.shape, jnp.bfloat16),
        ],
        in_specs=[whole_spec()] * (2 + len(flat)),
        out_specs=[whole_spec()] * 2,
        compiler_params=pltpu.CompilerParams(vmem_limit_bytes=FULL_VMEM),
    )(tokens, gain, *flat)


def pack_kernel(rows_ref, code_ref, out_ref, padded_ref):
    feature_dim = rows_ref.shape[1]
    main_width, piece = piece_widths(feature_dim)
    padded_ref[...] = jnp.zeros_like(padded_ref)
    padded_ref[:, :feature_dim] = rows_ref[...]
    for group in range(code_ref.shape[0]):
        codes = code_ref[group]
        slot = lax.broadcasted_iota(jnp.int32, codes.shape, 0) % MAIN
        fold = (codes.shape[0] // MAIN, MAIN, -1)
        out_ref[:, group, :, :main_width] = (
            dot32(as_bf16(codes == slot), padded_ref[:, :main_width])
            .reshape(fold)
            .astype(jnp.bfloat16)
        )
        tail = jnp.zeros((codes.shape[0], piece), jnp.float32)
        for j in range(MAIN):
            tail = tail + dot32(
                as_bf16((codes == MAIN) & (slot == j)), padded_ref[:, j * piece : (j + 1) * piece]
            )
        out_ref[:, group, :, main_width:] = tail.reshape(fold).astype(jnp.bfloat16)


def pack(rows, codes):
    main_width, piece = piece_widths(rows.shape[1])
    return pl.pallas_call(
        pack_kernel,
        out_shape=jax.ShapeDtypeStruct(
            (codes.shape[1] // MAIN, codes.shape[0], MAIN, main_width + piece), jnp.bfloat16
        ),
        in_specs=[whole_spec()] * 2,
        out_specs=whole_spec(),
        scratch_shapes=[pltpu.VMEM((rows.shape[0], MAIN * piece), jnp.bfloat16)],
        compiler_params=pltpu.CompilerParams(vmem_limit_bytes=FULL_VMEM),
    )(rows, codes)


def expert_kernel(feature_dim, x_ref, gate_ref, up_ref, down_ref, y_ref, x_all, total):
    main_width, piece = piece_widths(feature_dim)
    senders = x_ref.shape[0]
    main_rows = senders * MAIN
    step = pl.program_id(1) * pl.num_programs(2) + pl.program_id(2)
    last = pl.num_programs(1) * pl.num_programs(2) - 1

    @pl.when(step == 0)
    def _():
        x_all[:main_rows, :main_width] = x_ref[:, 0, :, :main_width].reshape(main_rows, main_width)
        row = lax.broadcasted_iota(jnp.int32, (senders, main_rows), 0)
        col = lax.broadcasted_iota(jnp.int32, (senders, main_rows), 1)
        tail = x_ref[:, 0, :, main_width:].reshape(main_rows, piece)
        for j in range(MAIN):
            x_all[main_rows:, j * piece : (j + 1) * piece] = dot32(
                as_bf16(col == row * MAIN + j), tail
            ).astype(jnp.bfloat16)

    x = x_all[:, :feature_dim]
    gate_part = dot32(x, gate_ref[0])
    up_part = dot32(x, up_ref[0])
    hidden_act = (gate_part * jax.nn.sigmoid(glu_alpha * gate_part) * (up_part + 1.0)).astype(
        jnp.bfloat16
    )
    product = lax.dot_general(
        hidden_act, down_ref[0], (((1,), (1,)), ((), ())), preferred_element_type=jnp.float32
    )

    @pl.when(step == 0)
    def _():
        total[...] = product

    @pl.when(step > 0)
    def _():
        total[...] += product

    @pl.when(step == last)
    def _():
        y_ref[:, 0, :, feature_dim:main_width] = jnp.zeros(
            (senders, MAIN, main_width - feature_dim), jnp.bfloat16
        )
        y_ref[:, 0, :, :feature_dim] = (
            total[:main_rows].reshape(senders, MAIN, feature_dim).astype(jnp.bfloat16)
        )
        x_all[main_rows:, :] = jnp.zeros((senders, MAIN * piece), jnp.bfloat16)
        x_all[main_rows:, :feature_dim] = total[main_rows:].astype(jnp.bfloat16)
        row = lax.broadcasted_iota(jnp.int32, (main_rows, senders), 0)
        col = lax.broadcasted_iota(jnp.int32, (main_rows, senders), 1)
        tail = jnp.zeros((main_rows, piece), jnp.float32)
        for j in range(MAIN):
            tail = tail + dot32(
                as_bf16(row == col * MAIN + j), x_all[main_rows:, j * piece : (j + 1) * piece]
            )
        y_ref[:, 0, :, main_width:] = tail.reshape(senders, MAIN, piece).astype(jnp.bfloat16)


def experts(x, expert_in, expert_out, halves):
    senders, groups, _, width = x.shape
    main_rows = senders * MAIN
    feature_dim, hidden_width = expert_in.shape[1], expert_out.shape[1]
    main_width, piece = piece_widths(feature_dim)
    rows = main_rows + main_rows // MAIN
    block = math.gcd(hidden_width, 768 if rows <= 512 else 128)
    steps = hidden_width // block
    slices = groups * halves
    return pl.pallas_call(
        lambda *refs: expert_kernel(feature_dim, *refs),
        grid=(groups, halves, steps),
        out_shape=jax.ShapeDtypeStruct(x.shape, jnp.bfloat16),
        in_specs=[
            pl.BlockSpec((senders, 1, MAIN, width), lambda g, j, f: (0, g, 0, 0)),
            pl.BlockSpec((1, feature_dim, block), lambda g, j, f: (g * halves + j, 0, f)),
            pl.BlockSpec((1, feature_dim, block), lambda g, j, f: (g * halves + j, 0, steps + f)),
            pl.BlockSpec((1, feature_dim, block), lambda g, j, f: (g * halves + j, 0, f)),
        ],
        out_specs=pl.BlockSpec((senders, 1, MAIN, width), lambda g, j, f: (0, g, 0, 0)),
        scratch_shapes=[
            pltpu.VMEM((rows, MAIN * piece), jnp.bfloat16),
            pltpu.VMEM((rows, feature_dim), jnp.float32),
        ],
        compiler_params=pltpu.CompilerParams(
            vmem_limit_bytes=FULL_VMEM, dimension_semantics=("arbitrary",) * 3
        ),
        cost_estimate=pl.CostEstimate(
            flops=6 * rows * feature_dim * hidden_width * slices,
            bytes_accessed=6 * feature_dim * hidden_width * slices,
            transcendentals=rows * hidden_width * slices,
        ),
    )(x, expert_in, expert_in, jnp.swapaxes(expert_out, 1, 2))


def combine_kernel(start_ref, back_ref, code_ref, weight_ref, out_ref):
    feature_dim = out_ref.shape[1]
    main_width, piece = piece_widths(feature_dim)
    senders, groups = back_ref.shape[:2]
    rows = senders * MAIN
    picks = []
    for group in range(groups):
        codes = code_ref[group]
        slot = lax.broadcasted_iota(jnp.int32, codes.shape, 1) % MAIN
        weights = weight_ref[group]
        high = weights.astype(jnp.bfloat16).astype(jnp.float32)
        picks.append((codes, slot, (high, weights - high)))

    def pick(group, chosen):
        codes, slot, parts = picks[group]
        condition = (codes == slot) if chosen is None else (codes == MAIN) & (slot == chosen)
        return [jnp.where(condition, part, 0.0).astype(jnp.bfloat16) for part in parts]

    main = [pick(group, None) for group in range(groups)]
    for j in range(MAIN):
        first, end = j * piece, min((j + 1) * piece, feature_dim)
        value = 0.0 if start_ref is None else start_ref[:, first:end]
        for group in range(groups):
            ninth = pick(group, j)
            tail = back_ref[:, group, :, main_width : main_width + end - first].reshape(rows, -1)
            part = back_ref[:, group, :, first:end].reshape(rows, -1)
            for k in range(2):
                value = value + dot32(main[group][k], part)
                value = value + dot32(ninth[k], tail)
        out_ref[:, first:end] = value.astype(out_ref.dtype)


def combine(start, back, codes, weights, feature_dim):
    alone = start is None
    given = (back, codes, weights) if alone else (start, back, codes, weights)
    return pl.pallas_call(
        (lambda *refs: combine_kernel(None, *refs)) if alone else combine_kernel,
        out_shape=jax.ShapeDtypeStruct(
            (codes.shape[1], feature_dim), jnp.bfloat16 if alone else jnp.float32
        ),
        in_specs=[whole_spec()] * len(given),
        out_specs=whole_spec(),
        compiler_params=pltpu.CompilerParams(vmem_limit_bytes=FULL_VMEM),
    )(*given)


def final_kernel(near_ref, far_ref, out_ref):
    out_ref[...] = (near_ref[...] + far_ref[...].astype(jnp.float32)).T.astype(out_ref.dtype)


def final_sum(near, far):
    rows, feature_dim = near.shape
    return pl.pallas_call(
        final_kernel,
        out_shape=jax.ShapeDtypeStruct((feature_dim, rows), jnp.bfloat16),
        in_specs=[whole_spec()] * 2,
        out_specs=whole_spec(),
        compiler_params=pltpu.CompilerParams(vmem_limit_bytes=FULL_VMEM),
    )(near, far).T


def mirrored(value):
    count = lax.axis_size("col")
    return lax.ppermute(value, "col", [(at, (at + count // 2) % count) for at in range(count)])


def exchange(value):
    rows, cols = lax.axis_size("row"), lax.axis_size("col")
    near = cols // 2
    halves = [
        [row * cols + side * near + at for row in range(rows) for at in range(near)]
        for side in (0, 1)
    ]
    return lax.all_to_all(
        value, ("row", "col"), split_axis=0, concat_axis=0, axis_index_groups=halves, tiled=True
    )


def shards(
    tokens,
    seg_ids,
    norm_gain,
    query_weight,
    kv_weight,
    out_weight,
    sinks,
    moe_gain,
    routes,
    route_weights,
    expert_in,
    expert_out,
):
    own_rows, feature_dim = tokens.shape
    row_count, col_count = lax.axis_size("row"), lax.axis_size("col")
    device_count = row_count * col_count
    row_at, col_at = lax.axis_index("row"), lax.axis_index("col")
    query_cols, kv_cols = query_weight.shape[1], kv_weight.shape[1]

    proj_weight = lax.all_gather(
        jnp.concatenate([query_weight, kv_weight], axis=1), "col", axis=0, tiled=True
    )
    out_cols = out_weight.shape[1]
    cut = up_to(2 * out_cols // 3, 8)
    out_parts = [
        lax.all_gather(part, "col", axis=1, tiled=True)
        for part in (out_weight[:, :cut], out_weight[:, cut:])
    ]

    normed = rms_scale(tokens, norm_gain).astype(jnp.bfloat16)
    block_x = jnp.zeros((row_count, own_rows, feature_dim), jnp.bfloat16)
    for distance in range(row_count):
        piece = swap_rows(normed, distance) if distance else normed
        block_x = lax.dynamic_update_index_in_dim(block_x, piece, row_at ^ distance, 0)
    block_rows = row_count * own_rows
    block_x = block_x.reshape(block_rows, feature_dim)

    all_segs = lax.all_to_all(
        jnp.broadcast_to(seg_ids[None, :], (device_count, own_rows)),
        ("col", "row"),
        split_axis=0,
        concat_axis=0,
        tiled=True,
    ).reshape(-1)
    base_index = col_at * block_rows
    padded_segs = jnp.concatenate([jnp.full((WIN,), -1, jnp.int32), all_segs])
    key_seg = lax.dynamic_slice_in_dim(padded_segs, base_index, WIN + block_rows, 0)
    block_seg = key_seg[WIN:]
    token_index = base_index + jnp.arange(block_rows, dtype=jnp.int32)
    starts = jnp.sum((all_segs[None, :] < block_seg[:, None]).astype(jnp.int32), axis=1)
    positions = token_index - starts

    slices_here = expert_in.shape[0]
    groups = max(1, slices_here // 2)
    halves = min(2, slices_here)
    near_cols = col_count // 2
    members = jnp.arange(row_count * near_cols, dtype=jnp.int32)
    member_at = (
        members // near_cols * col_count + members % near_cols + col_at // near_cols * near_cols
    )

    def slots(route_ids, weights_in):
        expert_ids = jnp.arange(EXPERTS, dtype=jnp.int32)
        named = route_ids[:, :, None] == expert_ids[None, None, :]
        hits = jnp.sum(named.astype(jnp.float32), axis=1)
        expert_weight = jnp.sum(jnp.where(named, weights_in[:, :, None], 0.0), axis=1)
        ranks = jnp.cumsum(hits, axis=0) - hits
        ranks = jnp.where(hits > 0, ranks, -1.0).astype(jnp.int32)
        code_in, code_out, weight_out = [], [], []
        for group in range(groups):
            chosen = member_at * slices_here // 2 + group
            spread = jnp.repeat(ranks[:, chosen], MAIN, axis=1)
            code_out.append(spread)
            code_in.append(spread.T)
            weight_out.append(jnp.repeat(expert_weight[:, chosen], MAIN, axis=1))
        return jnp.stack(code_in), jnp.stack(code_out), jnp.stack(weight_out)

    own_in, own_out, own_weight = slots(routes, route_weights)
    far_in, far_out, far_weight = slots(mirrored(routes), mirrored(route_weights))

    proj_weight, *codes = lax.optimization_barrier(
        (proj_weight, own_in, own_out, own_weight, far_in, far_out, far_weight)
    )
    own_in, own_out, own_weight, far_in, far_out, far_weight = codes
    proj_sum = dot32(block_x, proj_weight)
    query_sum, kv_sum = proj_sum[:, :query_cols], proj_sum[:, query_cols:]
    query_heads = query_cols // HD
    kv_heads = kv_cols // (2 * HD)
    group_size = query_heads // kv_heads
    queries = rotate(query_sum.reshape(block_rows, query_heads, HD), positions).astype(jnp.bfloat16)
    kv_pair = kv_sum.reshape(block_rows, kv_heads, 2, HD)
    keys = rotate(kv_pair[:, :, 0], positions).astype(jnp.bfloat16)
    values = kv_pair[:, :, 1].astype(jnp.bfloat16)
    kv_cache = jnp.stack([keys, values], axis=2).reshape(block_rows, kv_cols)
    edge_kv = from_behind(kv_cache[block_rows - WIN :], "col", 1)
    all_kv = jnp.concatenate([edge_kv, kv_cache], axis=0).reshape(WIN + block_rows, kv_heads, 2, HD)
    key_index = base_index - WIN + jnp.arange(WIN + block_rows, dtype=jnp.int32)
    query_grid = queries.reshape(block_rows, kv_heads, group_size, HD)
    sink_grid = sinks.reshape(kv_heads, group_size)
    attended = attend_tile(
        query_grid,
        all_kv[:, :, 0],
        all_kv[:, :, 1],
        block_seg,
        key_seg,
        token_index,
        key_index,
        sink_grid,
    ).reshape(block_rows, query_cols)

    sums = []
    for part in out_parts:
        if sums:
            part, sums = lax.optimization_barrier((part, sums))
        partial = dot32(attended, part).astype(jnp.bfloat16)
        partial = partial.reshape(row_count, own_rows, part.shape[1])
        pieces = []
        for distance in range(row_count):
            piece = lax.dynamic_index_in_dim(partial, row_at ^ distance, 0, False)
            pieces.append(swap_rows(piece, distance) if distance else piece)
        sums.append(pieces)

    hidden, moe_in = hidden_and_norm(
        tokens, moe_gain.reshape(1, feature_dim), sums, (cut, out_cols - cut)
    )
    far_rows = mirrored(moe_in)
    own_came = exchange(pack(moe_in, own_in))
    far_rows, own_came = lax.optimization_barrier((far_rows, own_came))
    far_came = exchange(pack(far_rows, far_in))
    own_made = experts(own_came, expert_in, expert_out, halves)
    far_came, own_made = lax.optimization_barrier((far_came, own_made))
    own_back = exchange(own_made)
    far_made = experts(far_came, expert_in, expert_out, halves)
    far_made, own_back = lax.optimization_barrier((far_made, own_back))
    far_back = exchange(far_made)
    near_sum = combine(hidden, own_back, own_out, own_weight, feature_dim)
    far_sum = mirrored(combine(None, far_back, far_out, far_weight, feature_dim))
    return (final_sum(near_sum, far_sum), kv_cache)


def solution(mesh):
    in_specs = (
        P(("col", "row"), None),
        P(("col", "row")),
        P(),
        P("col", "row"),
        P("col", "row"),
        P("row", "col"),
        P("row"),
        P(),
        P(("col", "row"), None),
        P(("col", "row"), None),
        P(("row", "col"), None, None),
        P(("row", "col"), None, None),
    )
    out_specs = (P(("col", "row"), None), P("col", "row"))
    return jax.shard_map(shards, mesh=mesh, in_specs=in_specs, out_specs=out_specs, check_vma=False)
```

```python
import math

import jax
import jax.numpy as jnp
from jax import lax
from jax.experimental import pallas as pl
from jax.experimental.pallas import tpu as pltpu
from jax.sharding import PartitionSpec as P

HD = 64
WIN = 128
EXPERTS = 64
TOP = 4
CAP = 9


eps_norm = 1e-05
theta_base = 150000.0
glu_alpha = 1.702
masked_score = -1e30


def from_behind(value, axis, steps):
    count = lax.axis_size(axis)
    first, last = (max(0, -steps), min(count, count - steps))
    return lax.ppermute(value, axis, [(source, source + steps) for source in range(first, last)])


def rms_scale(values_in, gain_vec):
    widened = values_in.astype(jnp.float32)
    return (
        widened
        * lax.rsqrt(jnp.mean(widened * widened, axis=-1, keepdims=True) + eps_norm)
        * gain_vec
    )


def rotate(values_in, positions):
    half_dim = values_in.shape[-1] // 2
    frequency = jnp.exp(
        jnp.arange(half_dim, dtype=jnp.float32)
        * (-2.0 * math.log(theta_base) / values_in.shape[-1])
    )
    angles = positions.astype(jnp.float32)[:, None] * frequency[None, :]
    cosine = jnp.cos(angles)[:, None, :]
    sine = jnp.sin(angles)[:, None, :]
    first_half = values_in[..., :half_dim]
    second_half = values_in[..., half_dim:]
    return jnp.concatenate(
        [first_half * cosine - second_half * sine, second_half * cosine + first_half * sine],
        axis=-1,
    )


def attend_tile(
    query_tile, key_tile, value_tile, query_seg, key_seg, query_pos, key_pos, sink_grid
):
    scores = jnp.einsum(
        "qkgd,lkd->kgql", query_tile, key_tile, preferred_element_type=jnp.float32
    ) * query_tile.shape[-1] ** (-0.5)
    distance = query_pos[:, None] - key_pos[None, :]
    allowed = (
        (query_seg[:, None] == key_seg[None, :])
        & (distance >= 0)
        & (distance < WIN)
        & (key_pos[None, :] >= 0)
    )
    scores = jnp.where(allowed[None, None], scores, masked_score)
    sink_col = sink_grid[:, :, None]
    ceiling = jnp.maximum(jnp.max(scores, axis=-1), sink_col)
    expo = jnp.exp(scores - ceiling[..., None])
    denom = jnp.sum(expo, axis=-1) + jnp.exp(sink_col - ceiling)
    probs = (expo / denom[..., None]).astype(jnp.bfloat16)
    return jnp.einsum(
        "kgql,lkd->qkgd", probs, value_tile, preferred_element_type=jnp.float32
    ).astype(jnp.bfloat16)


LANES = 128
MAIN = CAP - 1
FULL_VMEM = 56 * 1024 * 1024


def up_to(count, multiple):
    return -(-count // multiple) * multiple


def swap_rows(value, distance):
    count = lax.axis_size("row")
    return lax.ppermute(value, "row", [(place, place ^ distance) for place in range(count)])


def whole_spec():
    return pl.BlockSpec(memory_space=pltpu.VMEM)


def dot32(left, right):
    return jnp.dot(left, right, preferred_element_type=jnp.float32)


def piece_widths(feature_dim):
    piece = up_to(-(-feature_dim // MAIN), LANES)
    return up_to(feature_dim, LANES), piece


def as_bf16(condition):
    return jnp.where(condition, 1.0, 0.0).astype(jnp.bfloat16)


def hidden_kernel(counts, share, *refs):
    tokens_ref, gain_ref = refs[:2]
    part_refs, (hidden_ref, normed_ref) = refs[2:-2], refs[-2:]
    at = 0
    sums = []
    for count in counts:
        total = part_refs[at][...].astype(jnp.float32)
        for other in range(1, count):
            total = total + part_refs[at + other][...].astype(jnp.float32)
        at += count
        sums.append(total)
    pieces = []
    for block in range(tokens_ref.shape[1] // sum(share)):
        for size, total in zip(share, sums):
            pieces.append(total[:, block * size : (block + 1) * size])
    hidden = tokens_ref[...].astype(jnp.float32) + jnp.concatenate(pieces, axis=1)
    hidden_ref[...] = hidden
    scale = lax.rsqrt(jnp.mean(hidden * hidden, axis=-1, keepdims=True) + eps_norm)
    normed_ref[...] = (hidden * scale * gain_ref[...]).astype(jnp.bfloat16)


def hidden_and_norm(tokens, gain, parts, share):
    flat = [part for group in parts for part in group]
    return pl.pallas_call(
        lambda *refs: hidden_kernel(tuple(len(group) for group in parts), share, *refs),
        out_shape=[
            jax.ShapeDtypeStruct(tokens.shape, jnp.float32),
            jax.ShapeDtypeStruct(tokens.shape, jnp.bfloat16),
        ],
        in_specs=[whole_spec()] * (2 + len(flat)),
        out_specs=[whole_spec()] * 2,
        compiler_params=pltpu.CompilerParams(vmem_limit_bytes=FULL_VMEM),
    )(tokens, gain, *flat)


def pack_kernel(rows_ref, code_ref, out_ref, padded_ref):
    feature_dim = rows_ref.shape[1]
    main_width, piece = piece_widths(feature_dim)
    padded_ref[...] = jnp.zeros_like(padded_ref)
    padded_ref[:, :feature_dim] = rows_ref[...]
    for group in range(code_ref.shape[0]):
        codes = code_ref[group]
        slot = lax.broadcasted_iota(jnp.int32, codes.shape, 0) % MAIN
        fold = (codes.shape[0] // MAIN, MAIN, -1)
        out_ref[:, group, :, :main_width] = (
            dot32(as_bf16(codes == slot), padded_ref[:, :main_width])
            .reshape(fold)
            .astype(jnp.bfloat16)
        )
        tail = jnp.zeros((codes.shape[0], piece), jnp.float32)
        for j in range(MAIN):
            tail = tail + dot32(
                as_bf16((codes == MAIN) & (slot == j)), padded_ref[:, j * piece : (j + 1) * piece]
            )
        out_ref[:, group, :, main_width:] = tail.reshape(fold).astype(jnp.bfloat16)


def pack(rows, codes):
    main_width, piece = piece_widths(rows.shape[1])
    return pl.pallas_call(
        pack_kernel,
        out_shape=jax.ShapeDtypeStruct(
            (codes.shape[1] // MAIN, codes.shape[0], MAIN, main_width + piece), jnp.bfloat16
        ),
        in_specs=[whole_spec()] * 2,
        out_specs=whole_spec(),
        scratch_shapes=[pltpu.VMEM((rows.shape[0], MAIN * piece), jnp.bfloat16)],
        compiler_params=pltpu.CompilerParams(vmem_limit_bytes=FULL_VMEM),
    )(rows, codes)


def expert_kernel(feature_dim, x_ref, gate_ref, up_ref, down_ref, y_ref, x_all, total):
    main_width, piece = piece_widths(feature_dim)
    senders = x_ref.shape[0]
    main_rows = senders * MAIN
    step = pl.program_id(1) * pl.num_programs(2) + pl.program_id(2)
    last = pl.num_programs(1) * pl.num_programs(2) - 1

    @pl.when(step == 0)
    def _():
        x_all[:main_rows, :main_width] = x_ref[:, 0, :, :main_width].reshape(main_rows, main_width)
        row = lax.broadcasted_iota(jnp.int32, (senders, main_rows), 0)
        col = lax.broadcasted_iota(jnp.int32, (senders, main_rows), 1)
        tail = x_ref[:, 0, :, main_width:].reshape(main_rows, piece)
        for j in range(MAIN):
            x_all[main_rows:, j * piece : (j + 1) * piece] = dot32(
                as_bf16(col == row * MAIN + j), tail
            ).astype(jnp.bfloat16)

    x = x_all[:, :feature_dim]
    gate_part = dot32(x, gate_ref[0])
    up_part = dot32(x, up_ref[0])
    hidden_act = (gate_part * jax.nn.sigmoid(glu_alpha * gate_part) * (up_part + 1.0)).astype(
        jnp.bfloat16
    )
    product = lax.dot_general(
        hidden_act, down_ref[0], (((1,), (1,)), ((), ())), preferred_element_type=jnp.float32
    )

    @pl.when(step == 0)
    def _():
        total[...] = product

    @pl.when(step > 0)
    def _():
        total[...] += product

    @pl.when(step == last)
    def _():
        y_ref[:, 0, :, feature_dim:main_width] = jnp.zeros(
            (senders, MAIN, main_width - feature_dim), jnp.bfloat16
        )
        y_ref[:, 0, :, :feature_dim] = (
            total[:main_rows].reshape(senders, MAIN, feature_dim).astype(jnp.bfloat16)
        )
        x_all[main_rows:, :] = jnp.zeros((senders, MAIN * piece), jnp.bfloat16)
        x_all[main_rows:, :feature_dim] = total[main_rows:].astype(jnp.bfloat16)
        row = lax.broadcasted_iota(jnp.int32, (main_rows, senders), 0)
        col = lax.broadcasted_iota(jnp.int32, (main_rows, senders), 1)
        tail = jnp.zeros((main_rows, piece), jnp.float32)
        for j in range(MAIN):
            tail = tail + dot32(
                as_bf16(row == col * MAIN + j), x_all[main_rows:, j * piece : (j + 1) * piece]
            )
        y_ref[:, 0, :, main_width:] = tail.reshape(senders, MAIN, piece).astype(jnp.bfloat16)


def experts(x, expert_in, expert_out, halves):
    senders, groups, _, width = x.shape
    main_rows = senders * MAIN
    feature_dim, hidden_width = expert_in.shape[1], expert_out.shape[1]
    main_width, piece = piece_widths(feature_dim)
    rows = main_rows + main_rows // MAIN
    block = math.gcd(hidden_width, 768 if rows <= 512 else 128)
    steps = hidden_width // block
    slices = groups * halves
    return pl.pallas_call(
        lambda *refs: expert_kernel(feature_dim, *refs),
        grid=(groups, halves, steps),
        out_shape=jax.ShapeDtypeStruct(x.shape, jnp.bfloat16),
        in_specs=[
            pl.BlockSpec((senders, 1, MAIN, width), lambda g, j, f: (0, g, 0, 0)),
            pl.BlockSpec((1, feature_dim, block), lambda g, j, f: (g * halves + j, 0, f)),
            pl.BlockSpec((1, feature_dim, block), lambda g, j, f: (g * halves + j, 0, steps + f)),
            pl.BlockSpec((1, feature_dim, block), lambda g, j, f: (g * halves + j, 0, f)),
        ],
        out_specs=pl.BlockSpec((senders, 1, MAIN, width), lambda g, j, f: (0, g, 0, 0)),
        scratch_shapes=[
            pltpu.VMEM((rows, MAIN * piece), jnp.bfloat16),
            pltpu.VMEM((rows, feature_dim), jnp.float32),
        ],
        compiler_params=pltpu.CompilerParams(
            vmem_limit_bytes=FULL_VMEM, dimension_semantics=("arbitrary",) * 3
        ),
        cost_estimate=pl.CostEstimate(
            flops=6 * rows * feature_dim * hidden_width * slices,
            bytes_accessed=6 * feature_dim * hidden_width * slices,
            transcendentals=rows * hidden_width * slices,
        ),
    )(x, expert_in, expert_in, jnp.swapaxes(expert_out, 1, 2))


def combine_kernel(start_ref, back_ref, code_ref, weight_ref, out_ref):
    feature_dim = out_ref.shape[1]
    main_width, piece = piece_widths(feature_dim)
    senders, groups = back_ref.shape[:2]
    rows = senders * MAIN
    picks = []
    for group in range(groups):
        codes = code_ref[group]
        slot = lax.broadcasted_iota(jnp.int32, codes.shape, 1) % MAIN
        weights = weight_ref[group]
        high = weights.astype(jnp.bfloat16).astype(jnp.float32)
        picks.append((codes, slot, (high, weights - high)))

    def pick(group, chosen):
        codes, slot, parts = picks[group]
        condition = (codes == slot) if chosen is None else (codes == MAIN) & (slot == chosen)
        return [jnp.where(condition, part, 0.0).astype(jnp.bfloat16) for part in parts]

    main = [pick(group, None) for group in range(groups)]
    for j in range(MAIN):
        first, end = j * piece, min((j + 1) * piece, feature_dim)
        value = 0.0 if start_ref is None else start_ref[:, first:end]
        for group in range(groups):
            ninth = pick(group, j)
            tail = back_ref[:, group, :, main_width : main_width + end - first].reshape(rows, -1)
            part = back_ref[:, group, :, first:end].reshape(rows, -1)
            for k in range(2):
                value = value + dot32(main[group][k], part)
                value = value + dot32(ninth[k], tail)
        out_ref[:, first:end] = value.astype(out_ref.dtype)


def combine(start, back, codes, weights, feature_dim):
    alone = start is None
    given = (back, codes, weights) if alone else (start, back, codes, weights)
    return pl.pallas_call(
        (lambda *refs: combine_kernel(None, *refs)) if alone else combine_kernel,
        out_shape=jax.ShapeDtypeStruct(
            (codes.shape[1], feature_dim), jnp.bfloat16 if alone else jnp.float32
        ),
        in_specs=[whole_spec()] * len(given),
        out_specs=whole_spec(),
        compiler_params=pltpu.CompilerParams(vmem_limit_bytes=FULL_VMEM),
    )(*given)


def final_kernel(near_ref, far_ref, out_ref):
    out_ref[...] = (near_ref[...] + far_ref[...].astype(jnp.float32)).T.astype(out_ref.dtype)


def final_sum(near, far):
    rows, feature_dim = near.shape
    return pl.pallas_call(
        final_kernel,
        out_shape=jax.ShapeDtypeStruct((feature_dim, rows), jnp.bfloat16),
        in_specs=[whole_spec()] * 2,
        out_specs=whole_spec(),
        compiler_params=pltpu.CompilerParams(vmem_limit_bytes=FULL_VMEM),
    )(near, far).T


def mirrored(value):
    count = lax.axis_size("col")
    return lax.ppermute(value, "col", [(at, (at + count // 2) % count) for at in range(count)])


def exchange(value):
    rows, cols = lax.axis_size("row"), lax.axis_size("col")
    near = cols // 2
    halves = [
        [row * cols + side * near + at for row in range(rows) for at in range(near)]
        for side in (0, 1)
    ]
    return lax.all_to_all(
        value, ("row", "col"), split_axis=0, concat_axis=0, axis_index_groups=halves, tiled=True
    )


def shards(
    tokens,
    seg_ids,
    norm_gain,
    query_weight,
    kv_weight,
    out_weight,
    sinks,
    moe_gain,
    routes,
    route_weights,
    expert_in,
    expert_out,
):
    own_rows, feature_dim = tokens.shape
    row_count, col_count = lax.axis_size("row"), lax.axis_size("col")
    device_count = row_count * col_count
    row_at, col_at = lax.axis_index("row"), lax.axis_index("col")
    query_cols, kv_cols = query_weight.shape[1], kv_weight.shape[1]

    proj_weight = lax.all_gather(
        jnp.concatenate([query_weight, kv_weight], axis=1), "col", axis=0, tiled=True
    )
    out_cols = out_weight.shape[1]
    cut = up_to(2 * out_cols // 3, 8)
    out_parts = [
        lax.all_gather(part, "col", axis=1, tiled=True)
        for part in (out_weight[:, :cut], out_weight[:, cut:])
    ]

    normed = rms_scale(tokens, norm_gain).astype(jnp.bfloat16)
    block_x = jnp.zeros((row_count, own_rows, feature_dim), jnp.bfloat16)
    for distance in range(row_count):
        piece = swap_rows(normed, distance) if distance else normed
        block_x = lax.dynamic_update_index_in_dim(block_x, piece, row_at ^ distance, 0)
    block_rows = row_count * own_rows
    block_x = block_x.reshape(block_rows, feature_dim)

    all_segs = lax.all_to_all(
        jnp.broadcast_to(seg_ids[None, :], (device_count, own_rows)),
        ("col", "row"),
        split_axis=0,
        concat_axis=0,
        tiled=True,
    ).reshape(-1)
    base_index = col_at * block_rows
    padded_segs = jnp.concatenate([jnp.full((WIN,), -1, jnp.int32), all_segs])
    key_seg = lax.dynamic_slice_in_dim(padded_segs, base_index, WIN + block_rows, 0)
    block_seg = key_seg[WIN:]
    token_index = base_index + jnp.arange(block_rows, dtype=jnp.int32)
    starts = jnp.sum((all_segs[None, :] < block_seg[:, None]).astype(jnp.int32), axis=1)
    positions = token_index - starts

    slices_here = expert_in.shape[0]
    groups = max(1, slices_here // 2)
    halves = min(2, slices_here)
    near_cols = col_count // 2
    members = jnp.arange(row_count * near_cols, dtype=jnp.int32)
    member_at = (
        members // near_cols * col_count + members % near_cols + col_at // near_cols * near_cols
    )

    def slots(route_ids, weights_in):
        expert_ids = jnp.arange(EXPERTS, dtype=jnp.int32)
        named = route_ids[:, :, None] == expert_ids[None, None, :]
        hits = jnp.sum(named.astype(jnp.float32), axis=1)
        expert_weight = jnp.sum(jnp.where(named, weights_in[:, :, None], 0.0), axis=1)
        ranks = jnp.cumsum(hits, axis=0) - hits
        ranks = jnp.where(hits > 0, ranks, -1.0).astype(jnp.int32)
        code_in, code_out, weight_out = [], [], []
        for group in range(groups):
            chosen = member_at * slices_here // 2 + group
            spread = jnp.repeat(ranks[:, chosen], MAIN, axis=1)
            code_out.append(spread)
            code_in.append(spread.T)
            weight_out.append(jnp.repeat(expert_weight[:, chosen], MAIN, axis=1))
        return jnp.stack(code_in), jnp.stack(code_out), jnp.stack(weight_out)

    own_in, own_out, own_weight = slots(routes, route_weights)
    far_in, far_out, far_weight = slots(mirrored(routes), mirrored(route_weights))

    proj_weight, *codes = lax.optimization_barrier(
        (proj_weight, own_in, own_out, own_weight, far_in, far_out, far_weight)
    )
    own_in, own_out, own_weight, far_in, far_out, far_weight = codes
    proj_sum = dot32(block_x, proj_weight)
    query_sum, kv_sum = proj_sum[:, :query_cols], proj_sum[:, query_cols:]
    query_heads = query_cols // HD
    kv_heads = kv_cols // (2 * HD)
    group_size = query_heads // kv_heads
    queries = rotate(query_sum.reshape(block_rows, query_heads, HD), positions).astype(jnp.bfloat16)
    kv_pair = kv_sum.reshape(block_rows, kv_heads, 2, HD)
    keys = rotate(kv_pair[:, :, 0], positions).astype(jnp.bfloat16)
    values = kv_pair[:, :, 1].astype(jnp.bfloat16)
    kv_cache = jnp.stack([keys, values], axis=2).reshape(block_rows, kv_cols)
    edge_kv = from_behind(kv_cache[block_rows - WIN :], "col", 1)
    all_kv = jnp.concatenate([edge_kv, kv_cache], axis=0).reshape(WIN + block_rows, kv_heads, 2, HD)
    key_index = base_index - WIN + jnp.arange(WIN + block_rows, dtype=jnp.int32)
    query_grid = queries.reshape(block_rows, kv_heads, group_size, HD)
    sink_grid = sinks.reshape(kv_heads, group_size)
    attended = attend_tile(
        query_grid,
        all_kv[:, :, 0],
        all_kv[:, :, 1],
        block_seg,
        key_seg,
        token_index,
        key_index,
        sink_grid,
    ).reshape(block_rows, query_cols)

    sums = []
    for part in out_parts:
        if sums:
            part, sums = lax.optimization_barrier((part, sums))
        partial = dot32(attended, part).astype(jnp.bfloat16)
        partial = partial.reshape(row_count, own_rows, part.shape[1])
        pieces = []
        for distance in range(row_count):
            piece = lax.dynamic_index_in_dim(partial, row_at ^ distance, 0, False)
            pieces.append(swap_rows(piece, distance) if distance else piece)
        sums.append(pieces)

    hidden, moe_in = hidden_and_norm(
        tokens, moe_gain.reshape(1, feature_dim), sums, (cut, out_cols - cut)
    )
    far_rows = mirrored(moe_in)
    far_came = exchange(pack(far_rows, far_in))
    own_packed, far_came = lax.optimization_barrier((pack(moe_in, own_in), far_came))
    own_came = exchange(own_packed)
    far_made = experts(far_came, expert_in, expert_out, halves)
    own_came, far_made = lax.optimization_barrier((own_came, far_made))
    far_back = exchange(far_made)
    own_made = experts(own_came, expert_in, expert_out, halves)
    far_back, own_made = lax.optimization_barrier((far_back, own_made))
    far_sum = mirrored(combine(None, far_back, far_out, far_weight, feature_dim))
    near_sum = combine(hidden, exchange(own_made), own_out, own_weight, feature_dim)
    far_sum, near_sum = lax.optimization_barrier((far_sum, near_sum))
    return (final_sum(near_sum, far_sum), kv_cache)


def solution(mesh):
    in_specs = (
        P(("col", "row"), None),
        P(("col", "row")),
        P(),
        P("col", "row"),
        P("col", "row"),
        P("row", "col"),
        P("row"),
        P(),
        P(("col", "row"), None),
        P(("col", "row"), None),
        P(("row", "col"), None, None),
        P(("row", "col"), None, None),
    )
    out_specs = (P(("col", "row"), None), P("col", "row"))
    return jax.shard_map(shards, mesh=mesh, in_specs=in_specs, out_specs=out_specs, check_vma=False)
```
